128 devices in a mesh: au: 32 (over y, z, core), ia: 4 (over x).
Axes of the slice: x: 4, y: 4, z: 4, core: 2. Of those that a mesh axis runs over, the one named last changes fastest.
Arguments:
- tile_values: bfloat16 [32768, 128, 128], P(('au', 'ia')), may hold values from -6 to 6
- tile_index: int32 [3, 32768], P(None, ('au', 'ia')), may hold values from 0 to 31, as said below
- tile_count: int32 [128], P(('au', 'ia')), may hold values from 32 to 256, as said below
- user_prev: float32 [64, 131072], P(None, 'au')
- item_prev: float32 [64, 16384], P(None, 'ia')
- day_prior: float32 [64, 32], replicated, may hold values from -6 to 6
Outputs:
- user_factor: float32 [64, 131072], P(None, 'au')
- item_factor: float32 [64, 16384], P(None, 'ia')
- day_factor: float32 [64, 32], replicated
The draws below stay inside these ranges and needn't reach their ends.
Inputs may be any that keep to these rules, and one draw needn't show every extreme that they name: `tile_index`: row 0 is a user block among the 32 of the device's users, row 1 an item block among the 32 of its items, row 2 a day; slots at or past a device's count are ignored. `tile_count`: some device is full in every draw.
All inputs are finite; a program needn't handle non-finite values.
Results may differ from the reference program's by a relative error of at most 0.0016.
Values sent between devices are 32-bit elements; how exact they have to be, the bound alone decides.
A program may use at most 64 MiB of HBM per device.

```python
import math
import jax
import jax.numpy as jnp
from jax import lax

R = 64
TILE = 128
DAYS = 32
PASSES = 2
UB_DEV = 32
IB_DEV = 32
CAP = 256
USERS = 131072
ITEMS = 16384
DEVS = 128
SLOTS = 32768
N_AU = 32
N_IA = 4


def draw_tile_index(key, part):
    key = jax.random.fold_in(key, 11)
    first, second, third = jax.random.split(key, 3)
    user_blocks = jax.random.randint(first, (SLOTS,), 0, UB_DEV)
    item_blocks = jax.random.randint(second, (SLOTS,), 0, IB_DEV)
    day_numbers = jax.random.randint(third, (SLOTS,), 0, DAYS)
    return jnp.stack([user_blocks, item_blocks, day_numbers], 0).astype(jnp.int32)


def draw_tile_count(key, part):
    key = jax.random.fold_in(key, 12)
    first, second, third = jax.random.split(key, 3)
    counts = jax.random.randint(first, (DEVS,), max(1, CAP // 8), CAP // 2 + 1)
    crowded = jax.random.randint(second, (DEVS,), 0, 16) == 0
    counts = jnp.where(crowded, CAP, counts)
    fullest = jax.random.randint(third, (), 0, DEVS)
    counts = jnp.where(jnp.arange(DEVS) == fullest, CAP, counts)
    return counts.astype(jnp.int32)


def shaped_factor(key, noise, lowest, highest):
    mean_key, scale_key = jax.random.split(key)
    common = 0.6 * jax.random.normal(mean_key, (noise.shape[0], 1))
    spread = jnp.exp(jax.random.uniform(scale_key, (1, noise.shape[1]), minval=math.log(lowest), maxval=math.log(highest)))
    return ((noise + common) * spread).astype(jnp.float32)


def draw_user_prev(key, part):
    key = jax.random.fold_in(key, 13)
    noise_key, other_key = jax.random.split(key)
    noise = jax.random.normal(noise_key, (R, USERS))
    return shaped_factor(other_key, noise, 0.3, 3.0)


def draw_item_prev(key, part):
    key = jax.random.fold_in(key, 14)
    noise_key, other_key = jax.random.split(key)
    noise = jax.random.normal(noise_key, (R, ITEMS))
    return shaped_factor(other_key, noise, 0.3, 3.0)


def block_scale(stream_key, extent, shards, smallest, high):
    def one(dim, shards_of):
        draws = jax.random.uniform(jax.random.fold_in(jax.random.fold_in(stream_key, 6), dim), (shards_of,), jnp.float32, smallest / len(shards), high / len(shards))
        return jnp.repeat(jnp.exp(draws), extent[dim] // shards_of).reshape((-1,) + (1,) * (len(extent) - dim - 1))

    loudness = one(*shards[0])
    for cut in shards[1:]:
        loudness = loudness * one(*cut)
    return loudness


def bell_draw(rng, shape, width, most, cuts=(), kind=jnp.bfloat16):
    values = width * jax.random.normal(rng, shape, jnp.float32)
    if cuts:
        values = values * block_scale(rng, shape, cuts, -0.22, 0.18)
    return jnp.clip(values, -most, most).astype(kind)


def setup_inputs(seed: int = 0) -> dict:
    streams_of = jax.random.split(jax.random.key(seed), 7)
    return {
        "tile_values": bell_draw(streams_of[0], (SLOTS, TILE, TILE), 1.0, 6.0, ((0, 128),)),
        "tile_index": draw_tile_index(jax.random.fold_in(streams_of[6], 71), 0),
        "tile_count": draw_tile_count(jax.random.fold_in(streams_of[6], 71), 0),
        "user_prev": draw_user_prev(jax.random.fold_in(streams_of[6], 71), 0),
        "item_prev": draw_item_prev(jax.random.fold_in(streams_of[6], 71), 0),
        "day_prior": bell_draw(streams_of[5], (R, DAYS), 1.0, 6.0, (), jnp.float32),
    }


EPSILON = 1e-06
HIGHEST = lax.Precision.HIGHEST

def pick_blocks(rows, chosen):
    return jnp.take(rows.reshape(rows.shape[0], rows.shape[1] // TILE, TILE), chosen, axis=1)

def solve_rows(gram, rhs):
    components = gram.shape[0]
    matrix = gram / (jnp.trace(gram) / components) + 0.1 * jnp.eye(components, dtype=jnp.float32)
    lower = jnp.linalg.cholesky(matrix)
    return jax.scipy.linalg.cho_solve((lower, True), rhs)

def norm_scale(moments):
    return jnp.sqrt(jnp.mean(moments * moments) + EPSILON)

def gram_of(factor):
    return jnp.dot(factor, factor.T, precision=HIGHEST)

def rounded(values):
    return lax.optimization_barrier(values.astype(jnp.bfloat16)).astype(jnp.float32)

def day_part(tiles, chosen, alive, users, items):
    user_blocks = pick_blocks(rounded(users), chosen[0])
    item_blocks = pick_blocks(rounded(items), chosen[1])
    partial_value = jnp.einsum('rtu,tui->rti', user_blocks, tiles.astype(jnp.float32), precision=HIGHEST)
    weighed = lax.optimization_barrier(jnp.sum(partial_value * item_blocks, axis=2)) * alive[None, :]
    onehot = (chosen[2][:, None] == jnp.arange(DAYS, dtype=jnp.int32)[None, :]).astype(jnp.float32)
    return jnp.dot(weighed, onehot, precision=HIGHEST)

def user_part(tiles, chosen, alive, items, day_factor):
    scaled = rounded(pick_blocks(items, chosen[1]) * day_factor[:, chosen[2]][:, :, None])
    columns = jnp.einsum('rti,tui->rtu', scaled, tiles.astype(jnp.float32), precision=HIGHEST) * alive[None, :, None]
    onehot = (chosen[0][:, None] == jnp.arange(UB_DEV, dtype=jnp.int32)[None, :]).astype(jnp.float32)
    summed = jnp.einsum('rtu,tb->rbu', columns, onehot, precision=HIGHEST)
    return summed.reshape(summed.shape[0], UB_DEV * TILE)

def item_part(tiles, chosen, alive, users, day_factor):
    scaled = rounded(pick_blocks(users, chosen[0]) * day_factor[:, chosen[2]][:, :, None])
    columns = jnp.einsum('rtu,tui->rti', scaled, tiles.astype(jnp.float32), precision=HIGHEST) * alive[None, :, None]
    onehot = (chosen[1][:, None] == jnp.arange(IB_DEV, dtype=jnp.int32)[None, :]).astype(jnp.float32)
    summed = jnp.einsum('rti,tb->rbi', columns, onehot, precision=HIGHEST)
    return summed.reshape(summed.shape[0], IB_DEV * TILE)

def reference(tile_values, tile_index, tile_count, user_prev, item_prev, day_prior):
    device_count = N_AU * N_IA
    user_width = UB_DEV * TILE
    item_width = IB_DEV * TILE
    tiles_all = tile_values.reshape(device_count, CAP, TILE, TILE)
    chosen_all = tile_index.reshape(3, device_count, CAP).transpose(1, 0, 2)
    alive_all = (jnp.arange(CAP, dtype=jnp.int32)[None, :] < tile_count[:, None]).astype(jnp.float32)
    devices = jnp.arange(device_count, dtype=jnp.int32)

    def user_slice(users, device):
        return lax.dynamic_slice_in_dim(users, (device // N_IA * user_width).astype(jnp.int32), user_width, 1)

    def item_slice(items, device):
        return lax.dynamic_slice_in_dim(items, (device % N_IA * item_width).astype(jnp.int32), item_width, 1)

    def day_total(users, items):

        def visit(running, device):
            term = day_part(tiles_all[device], chosen_all[device], alive_all[device], user_slice(users, device), item_slice(items, device))
            return (running + term, None)
        return lax.scan(visit, jnp.zeros((R, DAYS), jnp.float32), devices)[0]

    def user_total(items, day_factor):

        def visit(running, device):
            term = user_part(tiles_all[device], chosen_all[device], alive_all[device], item_slice(items, device), day_factor)
            offset = (device // N_IA * user_width).astype(jnp.int32)
            before = lax.dynamic_slice_in_dim(running, offset, user_width, 1)
            return (lax.dynamic_update_slice_in_dim(running, before + term, offset, 1), None)
        return lax.scan(visit, jnp.zeros((R, USERS), jnp.float32), devices)[0]

    def item_total(users, day_factor):

        def visit(running, device):
            term = item_part(tiles_all[device], chosen_all[device], alive_all[device], user_slice(users, device), day_factor)
            offset = (device % N_IA * item_width).astype(jnp.int32)
            before = lax.dynamic_slice_in_dim(running, offset, item_width, 1)
            return (lax.dynamic_update_slice_in_dim(running, before + term, offset, 1), None)
        return lax.scan(visit, jnp.zeros((R, ITEMS), jnp.float32), devices)[0]
    users = user_prev
    items = item_prev
    gram_users = gram_of(users)
    gram_items = gram_of(items)
    day_factor = day_prior
    for turn in range(PASSES):
        moments = day_total(users, items)
        day_factor = solve_rows(gram_users * gram_items, moments / norm_scale(moments) + day_prior)
        gram_days = gram_of(day_factor)
        moments = user_total(items, day_factor)
        users = solve_rows(gram_items * gram_days, moments / norm_scale(moments) + user_prev)
        gram_users = gram_of(users)
        moments = item_total(users, day_factor)
        items = solve_rows(gram_users * gram_days, moments / norm_scale(moments) + item_prev)
        gram_items = gram_of(items)
    return (users, items, day_factor)
```

```python
import functools

import jax
import jax.numpy as jnp
from jax import lax
from jax.experimental import pallas as pl
from jax.experimental.pallas import tpu as pltpu
from jax.sharding import PartitionSpec as P

PASSES = 2
R = 64
TILE = 128
DAYS = 32
BLOCKS = 32
CAP = 256
EPSILON = 1e-06
USER_ENTRIES = 64 * 131072
ITEM_ENTRIES = 64 * 16384
UNROLL = 8
MESH = pl.DeviceIdType.MESH
F32 = jnp.float32
BF16 = jnp.bfloat16

SUMS = 1 + 3 * PASSES
SCALES = 2 * PASSES

NN = (((1,), (0,)), ((), ()))
NT = (((1,), (1,)), ((), ()))


def mm(left, right, dims=NN):
    return lax.dot_general(left, right, dims, preferred_element_type=F32)


def halves(values):
    high = values.astype(BF16)
    return high, (values - high.astype(F32)).astype(BF16)


def mm3(left, right, dims=NN):
    lh, ll = halves(left)
    rh, rl = halves(right)
    return mm(lh, rh, dims) + (mm(lh, rl, dims) + mm(ll, rh, dims))


def rounds(generators):
    generators = list(generators)
    while generators:
        generators = [one for one in generators if next(one, "end") != "end"]


class Copies:
    def __init__(self, send, recv):
        self.send, self.recv, self.used = send, recv, 0

    def start(self, source, target, device):
        copy = pltpu.make_async_remote_copy(
            src_ref=source,
            dst_ref=target,
            send_sem=self.send.at[self.used],
            recv_sem=self.recv.at[self.used],
            device_id=device,
            device_id_type=MESH,
        )
        self.used += 1
        copy.start()
        return copy


COPIES = 10 * (SUMS + SCALES) + PASSES * (6 + 6 + 2 * (1 + 6 + 3))


def kernel(
    codes, last, tiles_hbm, user_prior, item_prior, day_prior,
    user_out, item_out, day_out,
    tiles, running, users, items, users_half, items_half, spread,
    mu, mi, t1u, t1i, t2,
    slots, scale_slots, urecv, irecv_core, irecv_one, irecv_two,
    tile_sem, send, recv,
):
    au = lax.axis_index("au")
    x = lax.axis_index("ia")
    core = lax.rem(au, 2)
    z = lax.rem(lax.div(au, 2), 4)
    y = lax.div(au, 8)

    def at(yy, zz, cc):
        return (yy * 4 + zz) * 2 + cc

    def along_x(step):
        return (au, lax.rem(x + step, 4))

    def along_y(step):
        return (at(lax.rem(y + step, 4), z, core), x)

    def along_z(step):
        return (at(y, lax.rem(z + step, 4), core), x)

    twin = (at(y, z, 1 - core), x)
    one = y * (1 - core) + z * core
    two = z * (1 - core) + y * core

    def along_one(step):
        new = lax.rem(one + step, 4)
        return (at(new * (1 - core) + y * core, z * (1 - core) + new * core, core), x)

    def along_two(step):
        new = lax.rem(two + step, 4)
        return (at(y * (1 - core) + new * core, new * (1 - core) + z * core, core), x)

    copies = Copies(send, recv)

    tile_copy = pltpu.make_async_copy(tiles_hbm, tiles, tile_sem)
    tile_copy.start()

    barrier = pltpu.get_barrier_semaphore()
    peers = [twin]
    for step in (1, 2, 3):
        peers += [along_x(step), along_y(step), along_z(step)]
    for peer in peers:
        pl.semaphore_signal(barrier, inc=1, device_id=peer, device_id_type=MESH)

    def total_over_all(where, value, result):
        where[core] = value
        copy = copies.start(where.at[core], where.at[core], twin)
        yield
        copy.wait()
        value = where[0] + where[1]
        base = 2
        for mine, along in ((x, along_x), (y, along_y), (z, along_z)):
            where[base + mine] = value
            flying = [
                copies.start(where.at[base + mine], where.at[base + mine], along(step))
                for step in (1, 2, 3)
            ]
            yield
            for copy in flying:
                copy.wait()
            value = (where[base] + where[base + 1]) + (where[base + 2] + where[base + 3])
            base += 4
        result.append(value)

    def reduce_ring(source, mine, along, width, got):
        half = width // 2

        def part(share, second):
            return pl.ds(lax.rem(share, 4) * width + second * half, half)

        far, right, left = mine + 2, mine + 1, mine + 3
        c1 = copies.start(source.at[part(far, 0)], got.at[0], along(3))
        c2 = copies.start(source.at[part(far, 1)], got.at[1], along(1))
        c3 = copies.start(source.at[part(left, 1)], got.at[2], along(3))
        c4 = copies.start(source.at[part(right, 0)], got.at[3], along(1))
        yield
        c1.wait()
        source[part(left, 0)] = source[part(left, 0)] + got[0]
        c5 = copies.start(source.at[part(left, 0)], got.at[4], along(3))
        c2.wait()
        source[part(right, 1)] = source[part(right, 1)] + got[1]
        c6 = copies.start(source.at[part(right, 1)], got.at[5], along(1))
        yield
        for copy in (c3, c4, c5, c6):
            copy.wait()
        source[part(mine, 0)] = source[part(mine, 0)] + (got[4] + got[3])
        source[part(mine, 1)] = source[part(mine, 1)] + (got[2] + got[5])

    def gather_ring(source, mine, along, width):
        half = width // 2

        def part(share, second):
            ref = source.at[pl.ds(lax.rem(share, 4) * width + second * half, half)]
            return ref

        left, right = mine + 3, mine + 1
        c1 = copies.start(part(mine, 0), part(mine, 0), along(1))
        c2 = copies.start(part(mine, 1), part(mine, 1), along(3))
        c3 = copies.start(part(mine, 1), part(mine, 1), along(1))
        c4 = copies.start(part(mine, 0), part(mine, 0), along(3))
        yield
        c1.wait()
        c5 = copies.start(part(left, 0), part(left, 0), along(1))
        c2.wait()
        c6 = copies.start(part(right, 1), part(right, 1), along(3))
        yield
        for copy in (c3, c4, c5, c6):
            copy.wait()

    def reduce_direct(source, base, mine, along, got):
        flying = [
            copies.start(source.at[base + lax.rem(mine + step, 4)], got.at[step - 1], along(step))
            for step in (1, 2, 3)
        ]
        yield
        for copy in flying:
            copy.wait()
        source[base + mine] = source[base + mine] + (got[0] + got[1] + got[2])

    def gather_direct(source, base, mine, along):
        here = source.at[base + mine]
        flying = [copies.start(here, here, along(step)) for step in (1, 2, 3)]
        yield
        for copy in flying:
            copy.wait()

    def inverse(gram):
        rows = lax.broadcasted_iota(jnp.int32, (R, 2 * R), 0)
        lanes = lax.broadcasted_iota(jnp.int32, (R, 2 * R), 1)
        diagonal = jnp.where(rows == lanes, 1.0, 0.0)
        trace = jnp.sum(jnp.sum(gram * diagonal[:, :R], axis=1, keepdims=True), axis=0, keepdims=True)
        matrix = gram / (trace / R) + 0.1 * diagonal[:, :R]
        matrix = jnp.concatenate([matrix, diagonal[:, :R]], axis=1)

        def eight(_, matrix):
            for k in range(8):
                pivot = matrix[k : k + 1, k : k + 1]
                row = matrix[k : k + 1, :] / pivot
                column = matrix[:, k : k + 1] - jnp.where(rows[:, :1] == k, 1.0, 0.0)
                matrix = matrix - column * row
            matrix = jnp.concatenate([matrix[8:], matrix[:8]], axis=0)
            return pltpu.roll(matrix, 2 * R - 8, 1)

        return lax.fori_loop(0, R // 8, eight, matrix)[:, :R]

    def sweep(order, product, begin=0, end=CAP, acc=None):
        def visit(turn, acc):
            for k in range(UNROLL):
                place = turn * UNROLL + k
                code = codes[order, place]
                slot = code & 255
                ub = (code >> 8) & 31
                ib = (code >> 13) & 31
                day = (code >> 18) & 31
                keep = (1 - (code >> 23)).astype(F32)
                acc = acc * keep + product(tiles[slot], ub, ib, day)
                running[place] = acc
            return acc

        if acc is None:
            acc = jnp.zeros((R, TILE), F32)
        return lax.fori_loop(begin // UNROLL, end // UNROLL, visit, acc)

    def assemble(order, target):
        def visit(block, carry):
            target[block] = running[last[order, block]]
            return carry

        lax.fori_loop(0, BLOCKS, visit, 0)

    def gram_part(values):
        high, low = halves(values)
        cross = mm(high, low, NT)
        return mm(high, high, NT) + (cross + mm(low, high, NT))

    def user_gram_part():
        def visit(step, total):
            return total + gram_part(users[x * 8 + step])

        return lax.fori_loop(0, 8, visit, jnp.zeros((R, R), F32))

    def item_gram_part():
        return gram_part(items[core * 16 + one * 4 + two])

    def pair(left, right):
        return jnp.concatenate([left, right], axis=1)

    def squares(source, begin, count):
        total = jnp.zeros((8, TILE), F32)
        for step in range(count):
            value = source[begin + step]
            value = value * value
            total = total + jnp.sum(value.reshape(8, 8, TILE), axis=0)
        return total

    def scale_of(total, entries):
        total = jnp.sum(jnp.sum(total, axis=1, keepdims=True), axis=0, keepdims=True)
        return jnp.sqrt(total / entries + EPSILON)

    def prior_part(inv, prior):
        def visit(block, carry):
            t2[block] = mm3(inv, prior[:, pl.ds(pl.multiple_of(block * TILE, TILE), TILE)])
            return carry

        lax.fori_loop(0, BLOCKS, visit, 0)

    def apply(inv, source, begin, count, target):
        for step in range(count):
            target[begin + step] = mm3(inv, source[begin + step])

    def finish(target, target_half, t1, norm, out):
        def visit(block, carry):
            value = t1[block] / norm + t2[block]
            target[block] = value
            target_half[block] = value.astype(BF16)
            if out is not None:
                out[:, pl.ds(pl.multiple_of(block * TILE, TILE), TILE)] = value
            return carry

        lax.fori_loop(0, BLOCKS, visit, 0)

    def lay(block, carry):
        columns = pl.ds(pl.multiple_of(block * TILE, TILE), TILE)
        value = user_prior[:, columns]
        users[block] = value
        users_half[block] = value.astype(BF16)
        value = item_prior[:, columns]
        items[block] = value
        items_half[block] = value.astype(BF16)
        return carry

    lax.fori_loop(0, BLOCKS, lay, 0)
    running[CAP] = jnp.zeros((R, TILE), F32)
    first = pair(user_gram_part(), item_gram_part())

    pl.semaphore_wait(barrier, len(peers))
    found = []
    rounds([total_over_all(slots.at[0], first, found)])
    gram_users, gram_items = found[0][:, :R], found[0][:, R:]
    tile_copy.wait()

    for turn in range(PASSES):
        final = turn == PASSES - 1

        def day_product(tile, ub, ib, day):
            return mm(users_half[ub], tile) * items_half[ib].astype(F32)

        sweep(2, day_product)
        lanes = lax.broadcasted_iota(jnp.int32, (R, TILE), 1)

        def day_sum(day, total):
            value = jnp.sum(running[last[2, day]], axis=1, keepdims=True)
            return jnp.where(lanes == day, value, total)

        moments = lax.fori_loop(0, DAYS, day_sum, jnp.zeros((R, TILE), F32))
        found = []
        job = total_over_all(slots.at[1 + 3 * turn], moments, found)
        next(job)
        inv = inverse(gram_users * gram_items)
        rounds([job])
        moments = found[0][:, :DAYS]
        square = moments * moments
        square = jnp.sum(jnp.sum(square, axis=1, keepdims=True), axis=0, keepdims=True)
        norm = jnp.sqrt(square / (R * DAYS) + EPSILON)
        days = mm3(inv, moments / norm + day_prior[...])
        gram_days = gram_part(days)
        if final:
            day_out[...] = days
        for day in range(DAYS):
            spread[day] = jnp.broadcast_to(days[:, day : day + 1], (R, TILE))

        def user_product(tile, ub, ib, day):
            return mm((items[ib] * spread[day]).astype(BF16), tile, NT)

        sweep(0, user_product)
        assemble(0, mu)
        job = reduce_ring(mu, x, along_x, 8, urecv.at[turn])
        next(job)
        inv = inverse(gram_items * gram_days)
        next(job)
        prior_part(inv, user_prior)
        rounds([job])
        found = []
        apply(inv, mu, x * 8, 8, t1u.at[turn])
        rounds([
            gather_ring(t1u.at[turn], x, along_x, 8),
            total_over_all(scale_slots.at[2 * turn], squares(mu, x * 8, 8), found),
        ])
        finish(users, users_half, t1u.at[turn], scale_of(found[0], USER_ENTRIES), user_out if final else None)

        found = []
        job = total_over_all(slots.at[2 + 3 * turn], pair(user_gram_part(), jnp.zeros((R, R), F32)), found)
        next(job)

        def item_product(tile, ub, ib, day):
            return mm((users[ub] * spread[day]).astype(BF16), tile)

        sweep(1, item_product)
        assemble(1, mi)
        rounds([job])
        gram_users = found[0][:, :R]
        other = 16 - core * 16
        copy = copies.start(mi.at[pl.ds(other, 16)], irecv_core.at[turn], twin)
        inv = inverse(gram_users * gram_days)
        copy.wait()
        own = pl.ds(core * 16, 16)
        mi[own] = mi[own] + irecv_core[turn]
        job = reduce_ring(mi.at[own], one, along_one, 4, irecv_one.at[turn])
        next(job)
        prior_part(inv, item_prior)
        rounds([job])
        base = core * 16 + one * 4
        rounds([reduce_direct(mi, base, two, along_two, irecv_two.at[turn])])
        found = []
        apply(inv, mi, base + two, 1, t1i.at[turn])
        scale_job = total_over_all(scale_slots.at[2 * turn + 1], squares(mi, base + two, 1), found)
        next(scale_job)
        rounds([gather_direct(t1i.at[turn], base, two, along_two)])
        rounds([gather_ring(t1i.at[turn, own], one, along_one, 4), scale_job])
        copy = copies.start(t1i.at[turn, own], t1i.at[turn, own], twin)
        copy.wait()
        finish(items, items_half, t1i.at[turn], scale_of(found[0], ITEM_ENTRIES), item_out if final else None)
        if not final:
            found = []
            job = total_over_all(slots.at[3 + 3 * turn], pair(item_gram_part(), jnp.zeros((R, R), F32)), found)
            rounds([job])
            gram_items = found[0][:, :R]


def sorted_codes(tile_index, tile_count):
    slot = jnp.arange(CAP, dtype=jnp.int32)
    live = slot < tile_count[0]
    keys = jnp.where(live[None, :], tile_index, BLOCKS)
    unique = keys * CAP + slot[None, :]
    before = unique[:, None, :] < unique[:, :, None]
    same = keys[:, None, :] == keys[:, :, None]
    rank = jnp.sum(before.astype(jnp.int32), axis=2)
    follows = jnp.sum((before & same).astype(jnp.int32), axis=2) > 0
    code = slot + tile_index[0] * 256 + tile_index[1] * 8192 + tile_index[2] * 262144
    code = code[None, :] + jnp.where(follows, 0, 1 << 23)
    codes = jnp.sum(jnp.where(rank[:, None, :] == slot[None, :, None], code[:, None, :], 0), axis=2)
    block = jnp.arange(BLOCKS, dtype=jnp.int32)[None, :, None]
    upto = jnp.sum((keys[:, None, :] <= block).astype(jnp.int32), axis=2)
    count = jnp.sum((keys[:, None, :] == block).astype(jnp.int32), axis=2)
    return codes, jnp.where(count > 0, upto - 1, CAP)


def shards(tile_values, tile_index, tile_count, user_prev, item_prev, day_prior):
    codes, last = sorted_codes(tile_index, tile_count)
    vmem = pl.BlockSpec(memory_space=pltpu.VMEM)
    smem = pl.BlockSpec(memory_space=pltpu.SMEM)
    block = (BLOCKS, R, TILE)
    return pl.pallas_call(
        kernel,
        out_shape=(
            jax.ShapeDtypeStruct(user_prev.shape, F32),
            jax.ShapeDtypeStruct(item_prev.shape, F32),
            jax.ShapeDtypeStruct(day_prior.shape, F32),
        ),
        in_specs=[smem, smem, pl.BlockSpec(memory_space=pl.ANY), vmem, vmem, vmem],
        out_specs=(vmem, vmem, vmem),
        scratch_shapes=[
            pltpu.VMEM((CAP, TILE, TILE), BF16),
            pltpu.VMEM((CAP + 1, R, TILE), F32),
            pltpu.VMEM(block, F32),
            pltpu.VMEM(block, F32),
            pltpu.VMEM(block, BF16),
            pltpu.VMEM(block, BF16),
            pltpu.VMEM(block, F32),
            pltpu.VMEM(block, F32),
            pltpu.VMEM(block, F32),
            pltpu.VMEM((PASSES, *block), F32),
            pltpu.VMEM((PASSES, *block), F32),
            pltpu.VMEM(block, F32),
            pltpu.VMEM((SUMS, 14, R, TILE), F32),
            pltpu.VMEM((SCALES, 14, 8, TILE), F32),
            pltpu.VMEM((PASSES, 6, 4, R, TILE), F32),
            pltpu.VMEM((PASSES, 16, R, TILE), F32),
            pltpu.VMEM((PASSES, 6, 2, R, TILE), F32),
            pltpu.VMEM((PASSES, 3, R, TILE), F32),
            pltpu.SemaphoreType.DMA,
            pltpu.SemaphoreType.DMA((COPIES,)),
            pltpu.SemaphoreType.DMA((COPIES,)),
        ],
        compiler_params=pltpu.CompilerParams(
            collective_id=0, has_side_effects=True, vmem_limit_bytes=60 * 1024 * 1024
        ),
    )(codes, last, tile_values, user_prev, item_prev, day_prior)


def solution(mesh):
    return jax.shard_map(
        shards,
        mesh=mesh,
        in_specs=(
            P(("au", "ia"), None, None),
            P(None, ("au", "ia")),
            P(("au", "ia")),
            P(None, "au"),
            P(None, "ia"),
            P(),
        ),
        out_specs=(P(None, "au"), P(None, "ia"), P()),
        check_vma=False,
    )
```

```python
import functools

import jax
import jax.numpy as jnp
from jax import lax
from jax.experimental import pallas as pl
from jax.experimental.pallas import tpu as pltpu
from jax.sharding import PartitionSpec as P

PASSES = 2
R = 64
TILE = 128
DAYS = 32
BLOCKS = 32
CAP = 256
EPSILON = 1e-06
USER_ENTRIES = 64 * 131072
ITEM_ENTRIES = 64 * 16384
UNROLL = 32
MESH = pl.DeviceIdType.MESH
F32 = jnp.float32
BF16 = jnp.bfloat16

NN = (((1,), (0,)), ((), ()))
NT = (((1,), (1,)), ((), ()))


def mm(left, right, dims=NN):
    return lax.dot_general(left, right, dims, preferred_element_type=F32)


def halves(values):
    high = values.astype(BF16)
    return high, (values - high.astype(F32)).astype(BF16)


def left_three(values):
    high, low = halves(values)
    return jnp.concatenate([high, high, low], axis=1)


def right_three(values):
    high, low = halves(values)
    return jnp.concatenate([high, low, high], axis=0)


def drain(job):
    for _ in job:
        pass


class Copies:
    def __init__(self, send, recv):
        self.send, self.recv, self.used = send, recv, 0

    def start(self, source, target, device):
        copy = pltpu.make_async_remote_copy(
            src_ref=source,
            dst_ref=target,
            send_sem=self.send.at[self.used],
            recv_sem=self.recv.at[self.used],
            device_id=device,
            device_id_type=MESH,
        )
        self.used += 1
        copy.start()
        return copy


COPIES = 7 + 7 * (PASSES - 1) + 7 + 3 * PASSES + PASSES * (19 + 19 + 19 + 6 + 6 + 1 + 15 + 15 + 1)


def kernel(
    codes, last, tiles_hbm, user_prior, item_prior, day_prior,
    user_out, item_out, day_out,
    tiles, tiles_t, running, users, items, users_half, items_half, spread,
    mu, mi, t1u, t1i, t2,
    gu_slots, gv_slots, md_slots, scale_slots, urecv, irecv_core, irecv,
    tile_sem, send, recv,
):
    au = lax.axis_index("au")
    x = lax.axis_index("ia")
    core = lax.rem(au, 2)
    z = lax.rem(lax.div(au, 2), 4)
    y = lax.div(au, 8)
    plane = y * 4 + z

    def at(yy, zz, cc):
        return (yy * 4 + zz) * 2 + cc

    twin = (at(y, z, 1 - core), x)

    def along_x(step):
        return (au, lax.rem(x + step, 4))

    def along_y(step):
        return (at(lax.rem(y + step, 4), z, core), x)

    def along_z(step):
        return (at(y, lax.rem(z + step, 4), core), x)

    def along_yz(step):
        yy, zz = lax.rem(y + step // 4, 4), lax.rem(z + step % 4, 4)
        return (at(yy, zz, core), x)

    def plane_of(step):
        return lax.rem(y + step // 4, 4) * 4 + lax.rem(z + step % 4, 4)

    kinds = {
        "core": (2, core, lambda step: twin),
        "x": (4, x, along_x),
        "y": (4, y, along_y),
        "z": (4, z, along_z),
        "yz": (16, plane, along_yz),
    }

    copies = Copies(send, recv)

    tile_copy = pltpu.make_async_copy(tiles_hbm, tiles, tile_sem)
    tile_copy.start()

    barrier = pltpu.get_barrier_semaphore()
    peers = [twin] + [along_x(step) for step in (1, 2, 3)] + [along_yz(step) for step in range(1, 16)]
    for peer in peers:
        pl.semaphore_signal(barrier, inc=1, device_id=peer, device_id_type=MESH)

    def total_over(stages, where, value, result):
        base = 0
        for stage in stages:
            size, mine, along = kinds[stage]
            here = where.at[base + mine]
            where[base + mine] = value
            flying = [copies.start(here, here, along(step)) for step in range(1, size)]
            yield
            for copy in flying:
                copy.wait()
            terms = [where[base + place] for place in range(size)]
            while len(terms) > 1:
                terms = [terms[k] + terms[k + 1] for k in range(0, len(terms), 2)]
            value = terms[0]
            base += size
        result.append(value)

    def reduce_ring(source, mine, along, width, got):
        half = width // 2

        def part(share, second):
            return pl.ds(lax.rem(share, 4) * width + second * half, half)

        far, right, left = mine + 2, mine + 1, mine + 3
        c1 = copies.start(source.at[part(far, 0)], got.at[0], along(3))
        c2 = copies.start(source.at[part(far, 1)], got.at[1], along(1))
        c3 = copies.start(source.at[part(left, 1)], got.at[2], along(3))
        c4 = copies.start(source.at[part(right, 0)], got.at[3], along(1))
        yield
        c1.wait()
        source[part(left, 0)] = source[part(left, 0)] + got[0]
        c5 = copies.start(source.at[part(left, 0)], got.at[4], along(3))
        c2.wait()
        source[part(right, 1)] = source[part(right, 1)] + got[1]
        c6 = copies.start(source.at[part(right, 1)], got.at[5], along(1))
        yield
        for copy in (c3, c4, c5, c6):
            copy.wait()
        source[part(mine, 0)] = source[part(mine, 0)] + (got[4] + got[3])
        source[part(mine, 1)] = source[part(mine, 1)] + (got[2] + got[5])

    def gather_ring(source, mine, along, width):
        half = width // 2

        def part(share, second):
            return source.at[pl.ds(lax.rem(share, 4) * width + second * half, half)]

        left, right = mine + 3, mine + 1
        c1 = copies.start(part(mine, 0), part(mine, 0), along(1))
        c2 = copies.start(part(mine, 1), part(mine, 1), along(3))
        c3 = copies.start(part(mine, 1), part(mine, 1), along(1))
        c4 = copies.start(part(mine, 0), part(mine, 0), along(3))
        yield
        c1.wait()
        c5 = copies.start(part(left, 0), part(left, 0), along(1))
        c2.wait()
        c6 = copies.start(part(right, 1), part(right, 1), along(3))
        yield
        for copy in (c3, c4, c5, c6):
            copy.wait()

    def reduce_plane(source, base, got):
        flying = [
            copies.start(source.at[base + plane_of(step)], got.at[step - 1], along_yz(step))
            for step in range(1, 16)
        ]
        yield
        for copy in flying:
            copy.wait()
        total = source[base + plane]
        for step in range(15):
            total = total + got[step]
        source[base + plane] = total

    def gather_plane(source, base):
        here = source.at[base + plane]
        flying = [copies.start(here, here, along_yz(step)) for step in range(1, 16)]
        yield
        for copy in flying:
            copy.wait()

    def inverse(gram):
        rows = lax.broadcasted_iota(jnp.int32, (R, 2 * R), 0)
        lanes = lax.broadcasted_iota(jnp.int32, (R, 2 * R), 1)
        diagonal = jnp.where(rows == lanes, 1.0, 0.0)
        trace = jnp.sum(jnp.sum(gram * diagonal[:, :R], axis=1, keepdims=True), axis=0, keepdims=True)
        matrix = gram / (trace / R) + 0.1 * diagonal[:, :R]
        matrix = jnp.concatenate([matrix, diagonal[:, :R]], axis=1)

        def eight(_, matrix):
            for k in range(8):
                pivot = matrix[k : k + 1, k : k + 1]
                row = matrix[k : k + 1, :] / pivot
                column = matrix[:, k : k + 1] - jnp.where(rows[:, :1] == k, 1.0, 0.0)
                matrix = matrix - column * row
            matrix = jnp.concatenate([matrix[8:], matrix[:8]], axis=0)
            return pltpu.roll(matrix, 2 * R - 8, 1)

        return left_three(lax.fori_loop(0, R // 8, eight, matrix)[:, :R])

    def sweep(order, source, product, begin=0, end=CAP, acc=None):
        def visit(turn, acc):
            for k in range(UNROLL):
                place = turn * UNROLL + k
                code = codes[order, place]
                slot = code & 255
                ub = (code >> 8) & 31
                ib = (code >> 13) & 31
                day = (code >> 18) & 31
                keep = (1 - (code >> 23)).astype(F32)
                acc = acc * keep + product(source[slot], ub, ib, day)
                running[place] = acc
            return acc

        if acc is None:
            acc = jnp.zeros((R, TILE), F32)
        return lax.fori_loop(begin // UNROLL, end // UNROLL, visit, acc)

    def each_block(visit, by=4):
        def some(step, carry):
            for k in range(by):
                visit(step * by + k)
            return carry

        lax.fori_loop(0, BLOCKS // by, some, 0)

    def columns(block):
        return pl.ds(pl.multiple_of(block * TILE, TILE), TILE)

    def assemble(order, target):
        def visit(block):
            target[block] = running[last[order, block]]

        each_block(visit, 8)

    def gram_of(source):
        def four(step, carry):
            total, cross = carry
            for k in range(2):
                block = step * 4 + k * 2
                high, low = halves(jnp.concatenate([source[block], source[block + 1]], axis=1))
                total = total + mm(high, high, NT)
                cross = cross + mm(high, low, NT)
            return total, cross

        zero = jnp.zeros((R, R), F32)
        total, cross = lax.fori_loop(0, BLOCKS // 4, four, (zero, zero))
        return total + (cross + cross.T)

    def fold(gram):
        return jnp.concatenate([gram[: R // 2], gram[R // 2 :]], axis=1)

    def unfold(value):
        return jnp.concatenate([value[:, :R], value[:, R:]], axis=0)

    def squares(source, begin, count):
        total = jnp.zeros((8, TILE), F32)
        for step in range(count):
            value = source[begin + step]
            value = value * value
            total = total + jnp.sum(value.reshape(8, 8, TILE), axis=0)
        return total

    def scale_of(total, entries):
        total = jnp.sum(jnp.sum(total, axis=1, keepdims=True), axis=0, keepdims=True)
        return jnp.sqrt(total / entries + EPSILON)

    def prior_part(inv, prior):
        def visit(step, carry):
            wide = prior[:, pl.ds(pl.multiple_of(step * 4 * TILE, 4 * TILE), 4 * TILE)]
            wide = mm(inv, right_three(wide))
            for k in range(4):
                t2[step * 4 + k] = wide[:, k * TILE : (k + 1) * TILE]
            return carry

        lax.fori_loop(0, BLOCKS // 4, visit, 0)

    def apply(inv, source, begin, count, target):
        for step in range(count):
            target[begin + step] = mm(inv, right_three(source[begin + step]))

    def finish(target, target_half, t1, norm, out):
        share = 1.0 / norm

        def visit(block):
            value = t1[block] * share + t2[block]
            target[block] = value
            target_half[block] = value.astype(BF16)
            if out is not None:
                out[:, columns(block)] = value

        each_block(visit)

    def lay(block):
        value = user_prior[:, columns(block)]
        users[block] = value
        users_half[block] = value.astype(BF16)
        value = item_prior[:, columns(block)]
        items[block] = value
        items_half[block] = value.astype(BF16)

    each_block(lay)
    running[CAP] = jnp.zeros((R, TILE), F32)
    gu_part, gv_part = fold(gram_of(users)), fold(gram_of(items))
    day_rows = day_prior[...].T
    lanes = lax.broadcasted_iota(jnp.int32, (R, TILE), 1)

    def transpose_tiles(begin, end):
        def visit(step, carry):
            for k in range(16):
                tiles_t[step * 16 + k] = tiles[step * 16 + k].T
            return carry

        lax.fori_loop(begin // 16, end // 16, visit, 0)

    pl.semaphore_wait(barrier, len(peers))
    gu_found = []
    gu_job = total_over(("core", "y", "z"), gu_slots.at[0], gu_part, gu_found)
    next(gu_job)

    for turn in range(PASSES):
        final = turn == PASSES - 1

        gv_found = []
        gv_job = total_over(("x",), gv_slots.at[turn], gv_part, gv_found)
        next(gv_job)
        if turn == 0:
            tile_copy.wait()

        def day_product(tile, ub, ib, day):
            return mm(users_half[ub], tile) * items_half[ib].astype(F32)

        acc = sweep(2, tiles, day_product, 0, CAP // 2)
        if turn == 0:
            next(gu_job)
        sweep(2, tiles, day_product, CAP // 2, CAP, acc)

        def day_sums(step, total):
            for k in range(8):
                day = step * 8 + k
                value = jnp.sum(running[last[2, day]], axis=1, keepdims=True)
                total = jnp.where(lanes == day, value, total)
            return total

        moments = lax.fori_loop(0, DAYS // 8, day_sums, jnp.zeros((R, TILE), F32))
        moments = (moments[:16] + pltpu.roll(moments[16:32], 32, 1)) + (
            pltpu.roll(moments[32:48], 64, 1) + pltpu.roll(moments[48:], 96, 1)
        )
        md_found = []
        md_job = total_over(("core", "x", "yz"), md_slots.at[turn], moments, md_found)
        next(md_job)
        next(md_job)
        if turn == 0:
            next(gu_job)
            transpose_tiles(0, CAP // 2)
            next(md_job)
            transpose_tiles(CAP // 2, CAP)
            drain(gu_job)
            gram_users = unfold(gu_found[0])
            drain(gv_job)
            gram_items = unfold(gv_found[0])
            inv = inverse(gram_users * gram_items)
        else:
            drain(gv_job)
            gram_items = unfold(gv_found[0])
            inv = inverse(gram_users * gram_items)
            next(md_job)
        drain(md_job)
        moments = md_found[0]
        square = moments * moments
        square = jnp.sum(jnp.sum(square, axis=1, keepdims=True), axis=0, keepdims=True)
        norm = jnp.sqrt(square / (R * DAYS) + EPSILON)
        moments = moments / norm
        moments = jnp.concatenate(
            [moments[:, :DAYS]] + [pltpu.roll(moments, TILE - k * 32, 1)[:, :DAYS] for k in (1, 2, 3)], axis=0
        )
        days = mm(inv, right_three(moments + day_rows))
        for day in range(DAYS):
            spread[day] = jnp.broadcast_to(days[:, day : day + 1], (R, TILE))
        high, low = halves(days)
        cross = mm(high, low, NT)
        gram_days = mm(high, high, NT) + (cross + mm(low, high, NT))
        if final:
            day_out[...] = days.T

        def user_product(tile, ub, ib, day):
            return mm((items[ib] * spread[day]).astype(BF16), tile)

        sweep(0, tiles_t, user_product)
        assemble(0, mu)
        job = reduce_ring(mu, x, along_x, 8, urecv.at[turn])
        next(job)
        inv = inverse(gram_items * gram_days)
        drain(job)
        apply(inv, mu, x * 8, 8, t1u.at[turn])
        job = gather_ring(t1u.at[turn], x, along_x, 8)
        next(job)
        scale_found = []
        scale_job = total_over(
            ("core", "yz", "x"), scale_slots.at[turn, 0], squares(mu, x * 8, 8), scale_found
        )
        next(scale_job)
        next(scale_job)
        prior_part(inv, user_prior)
        next(job)
        next(scale_job)
        drain(scale_job)
        drain(job)
        finish(users, users_half, t1u.at[turn], scale_of(scale_found[0], USER_ENTRIES), user_out if final else None)

        gu_found = []
        gu_job = total_over(("core", "y", "z"), gu_slots.at[1 + turn], fold(gram_of(users)), gu_found)
        next(gu_job)

        def item_product(tile, ub, ib, day):
            return mm((users[ub] * spread[day]).astype(BF16), tile)

        acc = sweep(1, tiles, item_product, 0, CAP // 2)
        next(gu_job)
        sweep(1, tiles, item_product, CAP // 2, CAP, acc)
        assemble(1, mi)
        own, other = pl.ds(core * 16, 16), pl.ds(16 - core * 16, 16)
        copy = copies.start(mi.at[other], irecv_core.at[turn], twin)
        copy.wait()
        mi[own] = mi[own] + irecv_core[turn]
        job = reduce_plane(mi, core * 16, irecv.at[turn])
        next(job)
        drain(gu_job)
        gram_users = unfold(gu_found[0])
        inv = inverse(gram_users * gram_days)
        drain(job)
        apply(inv, mi, core * 16 + plane, 1, t1i.at[turn])
        job = gather_plane(t1i.at[turn], core * 16)
        next(job)
        scale_found = []
        scale_job = total_over(
            ("x", "yz", "core"), scale_slots.at[turn, 1], squares(mi, core * 16 + plane, 1), scale_found
        )
        next(scale_job)
        prior_part(inv, item_prior)
        next(scale_job)
        drain(job)
        copy = copies.start(t1i.at[turn, own], t1i.at[turn, own], twin)
        drain(scale_job)
        copy.wait()
        finish(items, items_half, t1i.at[turn], scale_of(scale_found[0], ITEM_ENTRIES), item_out if final else None)
        if not final:
            gv_part = fold(gram_of(items))


def sorted_codes(tile_index, tile_count):
    slot = jnp.arange(CAP, dtype=jnp.int32)
    live = slot < tile_count[0]
    keys = jnp.where(live[None, :], tile_index, BLOCKS)
    unique = keys * CAP + slot[None, :]
    before = unique[:, None, :] < unique[:, :, None]
    same = keys[:, None, :] == keys[:, :, None]
    rank = jnp.sum(before.astype(jnp.int32), axis=2)
    follows = jnp.sum((before & same).astype(jnp.int32), axis=2) > 0
    code = slot + tile_index[0] * 256 + tile_index[1] * 8192 + tile_index[2] * 262144
    code = code[None, :] + jnp.where(follows, 0, 1 << 23)
    codes = jnp.sum(jnp.where(rank[:, None, :] == slot[None, :, None], code[:, None, :], 0), axis=2)
    block = jnp.arange(BLOCKS, dtype=jnp.int32)[None, :, None]
    upto = jnp.sum((keys[:, None, :] <= block).astype(jnp.int32), axis=2)
    count = jnp.sum((keys[:, None, :] == block).astype(jnp.int32), axis=2)
    return codes, jnp.where(count > 0, upto - 1, CAP)


def shards(tile_values, tile_index, tile_count, user_prev, item_prev, day_prior):
    codes, last = sorted_codes(tile_index, tile_count)
    vmem = pl.BlockSpec(memory_space=pltpu.VMEM)
    smem = pl.BlockSpec(memory_space=pltpu.SMEM)
    block = (BLOCKS, R, TILE)
    users, items, days = pl.pallas_call(
        kernel,
        out_shape=(
            jax.ShapeDtypeStruct(user_prev.shape, F32),
            jax.ShapeDtypeStruct(item_prev.shape, F32),
            jax.ShapeDtypeStruct(day_prior.shape[::-1], F32),
        ),
        in_specs=[smem, smem, pl.BlockSpec(memory_space=pl.ANY), vmem, vmem, vmem],
        out_specs=(vmem, vmem, vmem),
        scratch_shapes=[
            pltpu.VMEM((CAP, TILE, TILE), BF16),
            pltpu.VMEM((CAP, TILE, TILE), BF16),
            pltpu.VMEM((CAP + 1, R, TILE), F32),
            pltpu.VMEM(block, F32),
            pltpu.VMEM(block, F32),
            pltpu.VMEM(block, BF16),
            pltpu.VMEM(block, BF16),
            pltpu.VMEM(block, F32),
            pltpu.VMEM(block, F32),
            pltpu.VMEM(block, F32),
            pltpu.VMEM((PASSES, *block), F32),
            pltpu.VMEM((PASSES, *block), F32),
            pltpu.VMEM(block, F32),
            pltpu.VMEM((1 + PASSES, 10, R // 2, 2 * R), F32),
            pltpu.VMEM((PASSES, 4, R // 2, 2 * R), F32),
            pltpu.VMEM((PASSES, 22, 16, TILE), F32),
            pltpu.VMEM((PASSES, 2, 22, 8, TILE), F32),
            pltpu.VMEM((PASSES, 6, 4, R, TILE), F32),
            pltpu.VMEM((PASSES, 16, R, TILE), F32),
            pltpu.VMEM((PASSES, 15, R, TILE), F32),
            pltpu.SemaphoreType.DMA,
            pltpu.SemaphoreType.DMA((COPIES,)),
            pltpu.SemaphoreType.DMA((COPIES,)),
        ],
        compiler_params=pltpu.CompilerParams(
            collective_id=0, has_side_effects=True, vmem_limit_bytes=60 * 1024 * 1024
        ),
    )(codes, last, tile_values, user_prev, item_prev, day_prior.T)
    return users, items, days.T


def solution(mesh):
    return jax.shard_map(
        shards,
        mesh=mesh,
        in_specs=(
            P(("au", "ia"), None, None),
            P(None, ("au", "ia")),
            P(("au", "ia")),
            P(None, "au"),
            P(None, "ia"),
            P(),
        ),
        out_specs=(P(None, "au"), P(None, "ia"), P()),
        check_vma=False,
    )
```

```python
import functools

import jax
import jax.numpy as jnp
from jax import lax
from jax.experimental import pallas as pl
from jax.experimental.pallas import tpu as pltpu
from jax.sharding import PartitionSpec as P

PASSES = 2
R = 64
TILE = 128
DAYS = 32
BLOCKS = 32
CAP = 256
EPSILON = 1e-06
USER_ENTRIES = 64 * 131072
ITEM_ENTRIES = 64 * 16384
UNROLL = 64
MESH = pl.DeviceIdType.MESH
F32 = jnp.float32
BF16 = jnp.bfloat16

NN = (((1,), (0,)), ((), ()))
NT = (((1,), (1,)), ((), ()))


def mm(left, right, dims=NN):
    return lax.dot_general(left, right, dims, preferred_element_type=F32)


def halves(values):
    high = values.astype(BF16)
    return high, (values - high.astype(F32)).astype(BF16)


def left_three(values):
    high, low = halves(values)
    return jnp.concatenate([high, high, low], axis=1)


def right_three(values):
    high, low = halves(values)
    return jnp.concatenate([high, low, high], axis=0)


def drain(job):
    for _ in job:
        pass


class Copies:
    def __init__(self, send, recv):
        self.send, self.recv, self.used = send, recv, 0

    def start(self, source, target, device):
        copy = pltpu.make_async_remote_copy(
            src_ref=source,
            dst_ref=target,
            send_sem=self.send.at[self.used],
            recv_sem=self.recv.at[self.used],
            device_id=device,
            device_id_type=MESH,
        )
        self.used += 1
        copy.start()
        return copy


COPIES = 7 + 7 * (PASSES - 1) + 7 + 3 * PASSES + PASSES * (19 + 19 + 19 + 12 + 12 + 4 + 15 + 15 + 4)


def kernel(
    codes, last, tiles_hbm, user_prior, item_prior, day_prior,
    user_out, item_out, day_out,
    tiles, tiles_t, running, users, items, users_half, items_half, spread,
    mu, mi, t1u, t1i, t2,
    gu_slots, gv_slots, md_slots, scale_slots, urecv, irecv_core, irecv,
    tile_sem, send, recv,
):
    au = lax.axis_index("au")
    x = lax.axis_index("ia")
    core = lax.rem(au, 2)
    z = lax.rem(lax.div(au, 2), 4)
    y = lax.div(au, 8)
    plane = y * 4 + z

    def at(yy, zz, cc):
        return (yy * 4 + zz) * 2 + cc

    twin = (at(y, z, 1 - core), x)

    def along_x(step):
        return (au, lax.rem(x + step, 4))

    def along_y(step):
        return (at(lax.rem(y + step, 4), z, core), x)

    def along_z(step):
        return (at(y, lax.rem(z + step, 4), core), x)

    def along_yz(step):
        yy, zz = lax.rem(y + step // 4, 4), lax.rem(z + step % 4, 4)
        return (at(yy, zz, core), x)

    def plane_of(step):
        return lax.rem(y + step // 4, 4) * 4 + lax.rem(z + step % 4, 4)

    kinds = {
        "core": (2, core, lambda step: twin),
        "x": (4, x, along_x),
        "y": (4, y, along_y),
        "z": (4, z, along_z),
        "yz": (16, plane, along_yz),
    }

    copies = Copies(send, recv)

    tile_copy = pltpu.make_async_copy(tiles_hbm, tiles, tile_sem)
    tile_copy.start()

    barrier = pltpu.get_barrier_semaphore()
    peers = [twin] + [along_x(step) for step in (1, 2, 3)] + [along_yz(step) for step in range(1, 16)]
    for peer in peers:
        pl.semaphore_signal(barrier, inc=1, device_id=peer, device_id_type=MESH)

    def total_over(stages, where, value, result):
        base = 0
        for stage in stages:
            size, mine, along = kinds[stage]
            here = where.at[base + mine]
            where[base + mine] = value
            flying = [copies.start(here, here, along(step)) for step in range(1, size)]
            yield
            for copy in flying:
                copy.wait()
            terms = [where[base + place] for place in range(size)]
            while len(terms) > 1:
                terms = [terms[k] + terms[k + 1] for k in range(0, len(terms), 2)]
            value = terms[0]
            base += size
        result.append(value)

    def ring_part(share, piece):
        return pl.ds(lax.rem(share, 4) * 8 + 2 * piece, 2)

    def reduce_ring(source, part, got):
        first, second = 2 * part, 2 * part + 1
        far, right, left = x + 2, x + 1, x + 3
        c1 = copies.start(source.at[ring_part(far, first)], got.at[0], along_x(3))
        c2 = copies.start(source.at[ring_part(far, second)], got.at[1], along_x(1))
        yield
        c3 = copies.start(source.at[ring_part(left, second)], got.at[2], along_x(3))
        c4 = copies.start(source.at[ring_part(right, first)], got.at[3], along_x(1))
        yield
        c1.wait()
        here = ring_part(left, first)
        source[here] = source[here] + got[0]
        c5 = copies.start(source.at[here], got.at[4], along_x(3))
        c2.wait()
        there = ring_part(right, second)
        source[there] = source[there] + got[1]
        c6 = copies.start(source.at[there], got.at[5], along_x(1))
        yield
        for copy in (c3, c4, c5, c6):
            copy.wait()
        mine = ring_part(x, first)
        source[mine] = source[mine] + (got[4] + got[3])
        mine = ring_part(x, second)
        source[mine] = source[mine] + (got[2] + got[5])

    def gather_ring(source, part):
        def piece(share, which):
            return source.at[ring_part(share, 2 * part + which)]

        left, right = x + 3, x + 1
        c1 = copies.start(piece(x, 0), piece(x, 0), along_x(1))
        c2 = copies.start(piece(x, 1), piece(x, 1), along_x(3))
        c3 = copies.start(piece(x, 1), piece(x, 1), along_x(1))
        c4 = copies.start(piece(x, 0), piece(x, 0), along_x(3))
        yield
        c1.wait()
        c5 = copies.start(piece(left, 0), piece(left, 0), along_x(1))
        c2.wait()
        c6 = copies.start(piece(right, 1), piece(right, 1), along_x(3))
        yield
        for copy in (c3, c4, c5, c6):
            copy.wait()

    def row_of(step):
        return pl.ds(lax.rem(y + step, 4) * 4, 4)

    def reduce_plane(source, got_core, got):
        own, other = core * 16, 16 - core * 16
        between = []
        for row in (2, 1, 3, 0):
            place = row_of(row)
            between.append((row, copies.start(source.at[pl.ds(other + place.start, 4)], got_core.at[place], twin)))
        yield
        flying = []
        for row, copy in between:
            copy.wait()
            place = row_of(row)
            here = pl.ds(own + place.start, 4)
            source[here] = source[here] + got_core[place]
            for step in range(row * 4, row * 4 + 4):
                if step:
                    flying.append(copies.start(source.at[own + plane_of(step)], got.at[step - 1], along_yz(step)))
        yield
        for copy in flying:
            copy.wait()
        total = source[own + plane]
        for step in range(15):
            total = total + got[step]
        source[own + plane] = total

    def gather_plane(source):
        own = core * 16
        here = source.at[own + plane]
        flying = {step: copies.start(here, here, along_yz(step)) for row in (2, 1, 3, 0) for step in range(row * 4, row * 4 + 4) if step}
        yield
        between = []
        for row in (0, 1, 3, 2):
            for step in range(row * 4, row * 4 + 4):
                if step:
                    flying[step].wait()
            place = source.at[pl.ds(own + row_of(4 - row).start, 4)]
            between.append(copies.start(place, place, twin))
        yield
        for copy in between:
            copy.wait()

    def inverse(gram):
        rows = lax.broadcasted_iota(jnp.int32, (R, 2 * R), 0)
        lanes = lax.broadcasted_iota(jnp.int32, (R, 2 * R), 1)
        diagonal = jnp.where(rows == lanes, 1.0, 0.0)
        trace = jnp.sum(jnp.sum(gram * diagonal[:, :R], axis=1, keepdims=True), axis=0, keepdims=True)
        matrix = gram / (trace / R) + 0.1 * diagonal[:, :R]
        matrix = jnp.concatenate([matrix, diagonal[:, :R]], axis=1)

        place = rows[:8]

        def wide(column):
            return jnp.broadcast_to(column, (8, 2 * R))

        def eight(_, matrix):
            top = matrix[:8]
            columns = [wide(top[:, k : k + 1]) for k in range(8)]
            for k in range(8):
                share = 1.0 / columns[k][k : k + 1]
                column = (columns[k] - jnp.where(place == k, 1.0, 0.0)) * share
                top = top - column * top[k : k + 1]
                for j in range(k + 1, 8):
                    columns[j] = columns[j] - column * columns[j][k : k + 1]
            rest = []
            for begin in range(8, R, 8):
                value = matrix[begin : begin + 8]
                terms = [wide(value[:, k : k + 1]) * top[k : k + 1] for k in range(8)]
                while len(terms) > 1:
                    terms = [terms[k] + terms[k + 1] for k in range(0, len(terms), 2)]
                rest.append(value - terms[0])
            return pltpu.roll(jnp.concatenate(rest + [top], axis=0), 2 * R - 8, 1)

        return left_three(lax.fori_loop(0, R // 8, eight, matrix)[:, :R])

    def sweep(order, source, product, begin=0, end=CAP, acc=None):
        def visit(turn, acc):
            for k in range(UNROLL):
                place = turn * UNROLL + k
                code = codes[order, place]
                slot = code & 255
                ub = (code >> 8) & 31
                ib = (code >> 13) & 31
                day = (code >> 18) & 31
                keep = (1 - (code >> 23)).astype(F32)
                acc = acc * keep + product(source[slot], ub, ib, day)
                running[place] = acc
            return acc

        if acc is None:
            acc = jnp.zeros((R, TILE), F32)
        return lax.fori_loop(begin // UNROLL, end // UNROLL, visit, acc)

    def each_block(visit, by=4, begin=0, count=BLOCKS):
        def some(step, carry):
            for k in range(by):
                visit(begin + step * by + k)
            return carry

        lax.fori_loop(0, count // by, some, 0)

    def columns(block):
        return pl.ds(pl.multiple_of(block * TILE, TILE), TILE)

    def assemble(order, target, begin=0, count=BLOCKS):
        def visit(block):
            target[block] = running[last[order, block]]

        each_block(visit, 8, begin, count)

    def gram_of(source):
        def four(step, carry):
            total, cross = carry
            for k in range(2):
                block = step * 4 + k * 2
                high, low = halves(jnp.concatenate([source[block], source[block + 1]], axis=1))
                total = total + mm(high, high, NT)
                cross = cross + mm(high, low, NT)
            return total, cross

        zero = jnp.zeros((R, R), F32)
        total, cross = lax.fori_loop(0, BLOCKS // 4, four, (zero, zero))
        return total + (cross + cross.T)

    def fold(gram):
        return jnp.concatenate([gram[: R // 2], gram[R // 2 :]], axis=1)

    def unfold(value):
        return jnp.concatenate([value[:, :R], value[:, R:]], axis=0)

    def squares(source, begin, count):
        total = jnp.zeros((8, TILE), F32)
        for step in range(count):
            value = source[begin + step]
            value = value * value
            total = total + jnp.sum(value.reshape(8, 8, TILE), axis=0)
        return total

    def scale_of(total, entries):
        total = jnp.sum(jnp.sum(total, axis=1, keepdims=True), axis=0, keepdims=True)
        return jnp.sqrt(total / entries + EPSILON)

    def prior_part(inv, prior):
        def visit(step, carry):
            wide = prior[:, pl.ds(pl.multiple_of(step * 4 * TILE, 4 * TILE), 4 * TILE)]
            wide = mm(inv, right_three(wide))
            for k in range(4):
                t2[step * 4 + k] = wide[:, k * TILE : (k + 1) * TILE]
            return carry

        lax.fori_loop(0, BLOCKS // 4, visit, 0)

    def apply(inv, source, begin, count, target):
        for step in range(count):
            target[begin + step] = mm(inv, right_three(source[begin + step]))

    def finish(target, target_half, t1, norm, out, begin=0, count=BLOCKS):
        share = 1.0 / norm

        def visit(block):
            value = t1[block] * share + t2[block]
            target[block] = value
            target_half[block] = value.astype(BF16)
            if out is not None:
                out[:, columns(block)] = value

        each_block(visit, 4, begin, count)

    def lay(block):
        value = user_prior[:, columns(block)]
        users[block] = value
        users_half[block] = value.astype(BF16)
        value = item_prior[:, columns(block)]
        items[block] = value
        items_half[block] = value.astype(BF16)

    each_block(lay)
    running[CAP] = jnp.zeros((R, TILE), F32)
    gu_part = fold(gram_of(users))
    day_rows = day_prior[...].T
    lanes = lax.broadcasted_iota(jnp.int32, (R, TILE), 1)

    def transpose_tiles(begin, end):
        def visit(step, carry):
            for k in range(16):
                tiles_t[step * 16 + k] = tiles[step * 16 + k].T
            return carry

        lax.fori_loop(begin // 16, end // 16, visit, 0)

    pl.semaphore_wait(barrier, len(peers))
    gu_found = []
    gu_job = total_over(("core", "y", "z"), gu_slots.at[0], gu_part, gu_found)
    next(gu_job)

    for turn in range(PASSES):
        final = turn == PASSES - 1

        if turn == 0:
            tile_copy.wait()

        def day_product(tile, ub, ib, day):
            return mm(users_half[ub], tile) * items_half[ib].astype(F32)

        acc = sweep(2, tiles, day_product, 0, CAP // 2)
        if turn == 0:
            next(gu_job)
        sweep(2, tiles, day_product, CAP // 2, CAP, acc)

        def day_sums(step, total):
            for k in range(8):
                day = step * 8 + k
                value = jnp.sum(running[last[2, day]], axis=1, keepdims=True)
                total = jnp.where(lanes == day, value, total)
            return total

        moments = lax.fori_loop(0, DAYS // 8, day_sums, jnp.zeros((R, TILE), F32))
        moments = (moments[:16] + pltpu.roll(moments[16:32], 32, 1)) + (
            pltpu.roll(moments[32:48], 64, 1) + pltpu.roll(moments[48:], 96, 1)
        )
        md_found = []
        md_job = total_over(("core", "x", "yz"), md_slots.at[turn], moments, md_found)
        next(md_job)
        gv_found = []
        gv_job = total_over(("x",), gv_slots.at[turn], fold(gram_of(items)), gv_found)
        next(gv_job)
        next(md_job)
        if turn == 0:
            next(gu_job)
            transpose_tiles(0, CAP // 2)
            next(md_job)
            transpose_tiles(CAP // 2, CAP)
            drain(gu_job)
            gram_users = unfold(gu_found[0])
            drain(gv_job)
            gram_items = unfold(gv_found[0])
            inv = inverse(gram_users * gram_items)
        else:
            drain(gv_job)
            gram_items = unfold(gv_found[0])
            next(md_job)
            inv = inverse(gram_users * gram_items)
        drain(md_job)
        moments = md_found[0]
        square = moments * moments
        square = jnp.sum(jnp.sum(square, axis=1, keepdims=True), axis=0, keepdims=True)
        norm = jnp.sqrt(square / (R * DAYS) + EPSILON)
        moments = moments / norm
        moments = jnp.concatenate(
            [moments[:, :DAYS]] + [pltpu.roll(moments, TILE - k * 32, 1)[:, :DAYS] for k in (1, 2, 3)], axis=0
        )
        days = mm(inv, right_three(moments + day_rows))
        for day in range(DAYS):
            spread[day] = jnp.broadcast_to(days[:, day : day + 1], (R, TILE))
        if final:
            day_out[...] = days.T

        def user_product(tile, ub, ib, day):
            return mm((items[ib] * spread[day]).astype(BF16), tile)

        sweep(0, tiles_t, user_product)
        assemble(0, mu)
        parts = [reduce_ring(mu, part, urecv.at[turn, part]) for part in range(2)]
        next(parts[0])
        next(parts[0])
        next(parts[1])
        high, low = halves(days)
        cross = mm(high, low, NT)
        gram_days = mm(high, high, NT) + (cross + mm(low, high, NT))
        inv = inverse(gram_items * gram_days)
        next(parts[0])
        next(parts[1])
        next(parts[1])
        jobs = []
        for part in range(2):
            drain(parts[part])
            apply(inv, mu, x * 8 + 4 * part, 4, t1u.at[turn])
            jobs.append(gather_ring(t1u.at[turn], part))
            next(jobs[part])
        scale_found = []
        scale_job = total_over(
            ("core", "yz", "x"), scale_slots.at[turn, 0], squares(mu, x * 8, 8), scale_found
        )
        next(scale_job)
        next(scale_job)
        prior_part(inv, user_prior)
        next(jobs[0])
        next(jobs[1])
        next(scale_job)
        drain(scale_job)
        for job in jobs:
            drain(job)
        finish(users, users_half, t1u.at[turn], scale_of(scale_found[0], USER_ENTRIES), user_out if final else None)

        gu_found = []
        gu_job = total_over(("core", "y", "z"), gu_slots.at[1 + turn], fold(gram_of(users)), gu_found)
        next(gu_job)

        def item_product(tile, ub, ib, day):
            return mm((users[ub] * spread[day]).astype(BF16), tile)

        acc = sweep(1, tiles, item_product, 0, CAP // 2)
        next(gu_job)
        sweep(1, tiles, item_product, CAP // 2, CAP, acc)
        assemble(1, mi, 16 - core * 16, 16)
        job = reduce_plane(mi, irecv_core.at[turn], irecv.at[turn])
        next(job)
        assemble(1, mi, core * 16, 16)
        next(job)
        drain(gu_job)
        gram_users = unfold(gu_found[0])
        inv = inverse(gram_users * gram_days)
        drain(job)
        apply(inv, mi, core * 16 + plane, 1, t1i.at[turn])
        job = gather_plane(t1i.at[turn])
        next(job)
        scale_found = []
        scale_job = total_over(
            ("x", "yz", "core"), scale_slots.at[turn, 1], squares(mi, core * 16 + plane, 1), scale_found
        )
        next(scale_job)
        prior_part(inv, item_prior)
        next(scale_job)
        next(job)
        drain(scale_job)
        norm = scale_of(scale_found[0], ITEM_ENTRIES)
        out = item_out if final else None
        finish(items, items_half, t1i.at[turn], norm, out, core * 16, 16)
        drain(job)
        finish(items, items_half, t1i.at[turn], norm, out, 16 - core * 16, 16)


def sorted_codes(tile_index, tile_count):
    slot = jnp.arange(CAP, dtype=jnp.int32)
    live = slot < tile_count[0]
    keys = jnp.where(live[None, :], tile_index, BLOCKS)
    unique = keys * CAP + slot[None, :]
    before = unique[:, None, :] < unique[:, :, None]
    same = keys[:, None, :] == keys[:, :, None]
    rank = jnp.sum(before.astype(jnp.int32), axis=2)
    follows = jnp.sum((before & same).astype(jnp.int32), axis=2) > 0
    code = slot + tile_index[0] * 256 + tile_index[1] * 8192 + tile_index[2] * 262144
    code = code[None, :] + jnp.where(follows, 0, 1 << 23)
    codes = jnp.sum(jnp.where(rank[:, None, :] == slot[None, :, None], code[:, None, :], 0), axis=2)
    block = jnp.arange(BLOCKS, dtype=jnp.int32)[None, :, None]
    upto = jnp.sum((keys[:, None, :] <= block).astype(jnp.int32), axis=2)
    count = jnp.sum((keys[:, None, :] == block).astype(jnp.int32), axis=2)
    return codes, jnp.where(count > 0, upto - 1, CAP)


def copy_kernel(user_in, item_in, day_in, user_out, item_out, day_out, sem):
    flying = [
        pltpu.make_async_copy(source, target, sem.at[k])
        for k, (source, target) in enumerate(((user_in, user_out), (item_in, item_out), (day_in, day_out)))
    ]
    for copy in flying:
        copy.start()
    for copy in flying:
        copy.wait()


def copied(arrays):
    anywhere = pl.BlockSpec(memory_space=pl.ANY)
    return pl.pallas_call(
        copy_kernel,
        out_shape=tuple(jax.ShapeDtypeStruct(one.shape, one.dtype) for one in arrays),
        in_specs=[anywhere] * 3,
        out_specs=(anywhere,) * 3,
        scratch_shapes=[pltpu.SemaphoreType.DMA((3,))],
    )(*arrays)


def shards(tile_values, tile_index, tile_count, user_prev, item_prev, day_prior):
    codes, last = sorted_codes(tile_index, tile_count)
    vmem = pl.BlockSpec(memory_space=pltpu.VMEM)
    smem = pl.BlockSpec(memory_space=pltpu.SMEM)
    block = (BLOCKS, R, TILE)
    results = pl.pallas_call(
        kernel,
        out_shape=(
            jax.ShapeDtypeStruct(user_prev.shape, F32),
            jax.ShapeDtypeStruct(item_prev.shape, F32),
            jax.ShapeDtypeStruct(day_prior.shape[::-1], F32),
        ),
        in_specs=[smem, smem, pl.BlockSpec(memory_space=pl.ANY), vmem, vmem, vmem],
        out_specs=(vmem, vmem, vmem),
        scratch_shapes=[
            pltpu.VMEM((CAP, TILE, TILE), BF16),
            pltpu.VMEM((CAP, TILE, TILE), BF16),
            pltpu.VMEM((CAP + 1, R, TILE), F32),
            pltpu.VMEM(block, F32),
            pltpu.VMEM(block, F32),
            pltpu.VMEM(block, BF16),
            pltpu.VMEM(block, BF16),
            pltpu.VMEM(block, F32),
            pltpu.VMEM(block, F32),
            pltpu.VMEM(block, F32),
            pltpu.VMEM((PASSES, *block), F32),
            pltpu.VMEM((PASSES, *block), F32),
            pltpu.VMEM(block, F32),
            pltpu.VMEM((1 + PASSES, 10, R // 2, 2 * R), F32),
            pltpu.VMEM((PASSES, 4, R // 2, 2 * R), F32),
            pltpu.VMEM((PASSES, 22, 16, TILE), F32),
            pltpu.VMEM((PASSES, 2, 22, 8, TILE), F32),
            pltpu.VMEM((PASSES, 2, 6, 2, R, TILE), F32),
            pltpu.VMEM((PASSES, 16, R, TILE), F32),
            pltpu.VMEM((PASSES, 15, R, TILE), F32),
            pltpu.SemaphoreType.DMA,
            pltpu.SemaphoreType.DMA((COPIES,)),
            pltpu.SemaphoreType.DMA((COPIES,)),
        ],
        compiler_params=pltpu.CompilerParams(
            collective_id=0, has_side_effects=True, vmem_limit_bytes=60 * 1024 * 1024
        ),
    )(codes, last, tile_values, user_prev, item_prev, day_prior.T)
    users, items, days = copied(results)
    return users, items, days.T


def solution(mesh):
    return jax.shard_map(
        shards,
        mesh=mesh,
        in_specs=(
            P(("au", "ia"), None, None),
            P(None, ("au", "ia")),
            P(("au", "ia")),
            P(None, "au"),
            P(None, "ia"),
            P(),
        ),
        out_specs=(P(None, "au"), P(None, "ia"), P()),
        check_vma=False,
    )
```

```python
import functools

import jax
import jax.numpy as jnp
from jax import lax
from jax.experimental import pallas as pl
from jax.experimental.pallas import tpu as pltpu
from jax.sharding import PartitionSpec as P

PASSES = 2
R = 64
TILE = 128
DAYS = 32
BLOCKS = 32
CAP = 256
EPSILON = 1e-06
USER_ENTRIES = 64 * 131072
ITEM_ENTRIES = 64 * 16384
UNROLL = 64
MESH = pl.DeviceIdType.MESH
F32 = jnp.float32
BF16 = jnp.bfloat16

NN = (((1,), (0,)), ((), ()))
NT = (((1,), (1,)), ((), ()))


def mm(left, right, dims=NN):
    return lax.dot_general(left, right, dims, preferred_element_type=F32)


def halves(values):
    high = values.astype(BF16)
    return high, (values - high.astype(F32)).astype(BF16)


def left_three(values):
    high, low = halves(values)
    return jnp.concatenate([high, high, low], axis=1)


def right_three(values):
    high, low = halves(values)
    return jnp.concatenate([high, low, high], axis=0)


def drain(job):
    for _ in job:
        pass


class Group:
    def __init__(self, sems):
        self.send, self.recv = sems

    def start(self, source, target, device):
        pltpu.make_async_remote_copy(
            src_ref=source,
            dst_ref=target,
            send_sem=self.send,
            recv_sem=self.recv,
            device_id=device,
            device_id_type=MESH,
        ).start()

    def wait(self, all_of_it):
        pltpu.make_async_copy(all_of_it, all_of_it, self.recv).wait()
        pltpu.make_async_copy(all_of_it, all_of_it, self.send).wait()


class Groups:
    def __init__(self, send, recv):
        self.send, self.recv, self.used = send, recv, 0

    def new(self):
        self.used += 1
        return Group((self.send.at[self.used - 1], self.recv.at[self.used - 1]))


GROUPS = 3 + PASSES * (3 + 1 + 3 + 3 + 3 + 4 + 4 + 4 + 1 + 4 + 1)


def order_slots(index, live, codes, last):
    slot = lax.broadcasted_iota(jnp.int32, (8, CAP), 1)
    rows = jnp.concatenate([index[...], jnp.zeros((5, CAP), jnp.int32)], axis=0)
    keys = jnp.where(slot < live, rows, BLOCKS)
    unique = keys * CAP + slot
    unique_down = unique.T
    code = slot[:1] + rows[:1] * 256 + rows[1:2] * 8192 + rows[2:3] * 262144
    ranks = [
        jnp.sum(jnp.where(unique_down[:, k : k + 1] < unique[k : k + 1], 1, 0), axis=0, keepdims=True)
        for k in range(3)
    ]
    down = jnp.concatenate(ranks + [code, slot[:4]], axis=0).T
    keys_down = keys.T
    place = lax.broadcasted_iota(jnp.int32, (CAP, CAP), 1)
    block = lax.broadcasted_iota(jnp.int32, (CAP, TILE), 1)
    for k in range(3):
        chosen = jnp.where(down[:, k : k + 1] == place, down[:, 3:4], 0)
        chosen = jnp.sum(chosen, axis=0, keepdims=True)
        key = jnp.where(slot[:1] < live, (chosen >> (8 + 5 * k)) & 31, BLOCKS)
        starts = (slot[:1] == 0) | (key != pltpu.roll(key, 1, 1))
        codes[k : k + 1, :] = chosen + jnp.where(starts, 1 << 23, 0)
        upto = jnp.sum(jnp.where(keys_down[:, k : k + 1] <= block, 1, 0), axis=0, keepdims=True)
        count = jnp.sum(jnp.where(keys_down[:, k : k + 1] == block, 1, 0), axis=0, keepdims=True)
        last[k : k + 1, :] = jnp.where(count > 0, upto - 1, CAP)


def kernel(
    index, live_count, tiles_hbm, user_hbm, item_hbm, day_prior,
    user_out, item_out, day_out,
    user_prior, item_prior,
    tiles, tiles_t, running, users, items, users_half, items_half, spread,
    mu, mi, t1u, t1i, t2,
    gu_slots, gv_slots, md_slots, scale_slots, urecv, irecv_core, irecv,
    codes_made, last_made, codes, last,
    tile_sem, prior_sem, out_sem, order_sem, send, recv,
):
    au = lax.axis_index("au")
    x = lax.axis_index("ia")
    core = lax.rem(au, 2)
    z = lax.rem(lax.div(au, 2), 4)
    y = lax.div(au, 8)
    plane = y * 4 + z

    def at(yy, zz, cc):
        return (yy * 4 + zz) * 2 + cc

    twin = (at(y, z, 1 - core), x)

    def along_x(step):
        return (au, lax.rem(x + step, 4))

    def along_y(step):
        return (at(lax.rem(y + step, 4), z, core), x)

    def along_z(step):
        return (at(y, lax.rem(z + step, 4), core), x)

    def along_yz(step):
        yy, zz = lax.rem(y + step // 4, 4), lax.rem(z + step % 4, 4)
        return (at(yy, zz, core), x)

    def plane_of(step):
        return lax.rem(y + step // 4, 4) * 4 + lax.rem(z + step % 4, 4)

    kinds = {
        "core": (2, core, lambda step: twin),
        "x": (4, x, along_x),
        "y": (4, y, along_y),
        "z": (4, z, along_z),
        "yz": (16, plane, along_yz),
    }

    groups = Groups(send, recv)

    tile_copy = pltpu.make_async_copy(tiles_hbm, tiles, tile_sem)
    prior_copies = [
        pltpu.make_async_copy(user_hbm, user_prior, prior_sem.at[0]),
        pltpu.make_async_copy(item_hbm, item_prior, prior_sem.at[1]),
    ]
    for copy in prior_copies:
        copy.start()
    tile_copy.start()

    barrier = pltpu.get_barrier_semaphore()
    peers = [twin] + [along_x(step) for step in (1, 2, 3)] + [along_yz(step) for step in range(1, 16)]
    for peer in peers:
        pl.semaphore_signal(barrier, inc=1, device_id=peer, device_id_type=MESH)

    def total_over(stages, where, value, result):
        base = 0
        for stage in stages:
            size, mine, along = kinds[stage]
            here = where.at[base + mine]
            where[base + mine] = value
            group = groups.new()
            for step in range(1, size):
                group.start(here, here, along(step))
            yield
            group.wait(where.at[pl.ds(base, size - 1)])
            terms = [where[base + place] for place in range(size)]
            while len(terms) > 1:
                terms = [terms[k] + terms[k + 1] for k in range(0, len(terms), 2)]
            value = terms[0]
            base += size
        result.append(value)

    def ring_part(share, piece):
        return pl.ds(lax.rem(share, 4) * 8 + 2 * piece, 2)

    def reduce_ring(source, part, got):
        first, second = 2 * part, 2 * part + 1
        far, right, left = x + 2, x + 1, x + 3
        distant, close = groups.new(), groups.new()
        distant.start(source.at[ring_part(far, first)], got.at[0], along_x(3))
        distant.start(source.at[ring_part(far, second)], got.at[1], along_x(1))
        yield
        close.start(source.at[ring_part(left, second)], got.at[2], along_x(3))
        close.start(source.at[ring_part(right, first)], got.at[3], along_x(1))
        yield
        distant.wait(got.at[pl.ds(0, 2)])
        here = ring_part(left, first)
        source[here] = source[here] + got[0]
        close.start(source.at[here], got.at[4], along_x(3))
        there = ring_part(right, second)
        source[there] = source[there] + got[1]
        close.start(source.at[there], got.at[5], along_x(1))
        yield
        close.wait(got.at[pl.ds(2, 4)])
        mine = ring_part(x, first)
        source[mine] = source[mine] + (got[4] + got[3])
        mine = ring_part(x, second)
        source[mine] = source[mine] + (got[2] + got[5])

    def gather_ring(source, part):
        def piece(share, which):
            return source.at[ring_part(share, 2 * part + which)]

        left, right = x + 3, x + 1
        onward, rest = groups.new(), groups.new()
        onward.start(piece(x, 0), piece(x, 0), along_x(1))
        onward.start(piece(x, 1), piece(x, 1), along_x(3))
        rest.start(piece(x, 1), piece(x, 1), along_x(1))
        rest.start(piece(x, 0), piece(x, 0), along_x(3))
        yield
        onward.wait(source.at[pl.ds(0, 4)])
        rest.start(piece(left, 0), piece(left, 0), along_x(1))
        rest.start(piece(right, 1), piece(right, 1), along_x(3))
        yield
        rest.wait(source.at[pl.ds(0, 8)])

    def row_of(step):
        return pl.ds(lax.rem(y + step, 4) * 4, 4)

    def reduce_plane(source, got_core, got):
        own, other = core * 16, 16 - core * 16
        between = []
        for row in (2, 1, 3, 0):
            place = row_of(row)
            group = groups.new()
            group.start(source.at[pl.ds(other + place.start, 4)], got_core.at[place], twin)
            between.append((row, group))
        yield
        flying = groups.new()
        for row, group in between:
            place = row_of(row)
            group.wait(got_core.at[place])
            here = pl.ds(own + place.start, 4)
            source[here] = source[here] + got_core[place]
            for step in range(row * 4, row * 4 + 4):
                if step:
                    flying.start(source.at[own + plane_of(step)], got.at[step - 1], along_yz(step))
        yield
        flying.wait(got)
        total = source[own + plane]
        for step in range(15):
            total = total + got[step]
        source[own + plane] = total

    def gather_plane(source):
        own = core * 16
        here = source.at[own + plane]
        flying = {row: groups.new() for row in range(4)}
        for row in (2, 1, 3, 0):
            for step in range(row * 4, row * 4 + 4):
                if step:
                    flying[row].start(here, here, along_yz(step))
        yield
        between = groups.new()
        for row in (0, 1, 3, 2):
            flying[row].wait(source.at[pl.ds(0, 4 if row else 3)])
            place = source.at[pl.ds(own + row_of(4 - row).start, 4)]
            between.start(place, place, twin)
        yield
        between.wait(source.at[pl.ds(0, 16)])

    def inverse(gram):
        rows = lax.broadcasted_iota(jnp.int32, (R, 2 * R), 0)
        lanes = lax.broadcasted_iota(jnp.int32, (R, 2 * R), 1)
        diagonal = jnp.where(rows == lanes, 1.0, 0.0)
        trace = jnp.sum(jnp.sum(gram * diagonal[:, :R], axis=1, keepdims=True), axis=0, keepdims=True)
        matrix = gram / (trace / R) + 0.1 * diagonal[:, :R]
        matrix = jnp.concatenate([matrix, diagonal[:, :R]], axis=1)

        place = rows[:8]

        def wide(column):
            return jnp.broadcast_to(column, (8, 2 * R))

        def eight(_, matrix):
            top = matrix[:8]
            columns = [wide(top[:, k : k + 1]) for k in range(8)]
            for k in range(8):
                share = 1.0 / columns[k][k : k + 1]
                column = (columns[k] - jnp.where(place == k, 1.0, 0.0)) * share
                top = top - column * top[k : k + 1]
                for j in range(k + 1, 8):
                    columns[j] = columns[j] - column * columns[j][k : k + 1]
            rest = []
            for begin in range(8, R, 8):
                value = matrix[begin : begin + 8]
                terms = [wide(value[:, k : k + 1]) * top[k : k + 1] for k in range(8)]
                while len(terms) > 1:
                    terms = [terms[k] + terms[k + 1] for k in range(0, len(terms), 2)]
                rest.append(value - terms[0])
            return pltpu.roll(jnp.concatenate(rest + [top], axis=0), 2 * R - 8, 1)

        return left_three(lax.fori_loop(0, R // 8, eight, matrix)[:, :R])

    def sweep(order, source, product, begin=0, end=CAP, acc=None):
        def visit(turn, acc):
            for k in range(UNROLL):
                place = turn * UNROLL + k
                code = codes[order, place]
                slot = code & 255
                ub = (code >> 8) & 31
                ib = (code >> 13) & 31
                day = (code >> 18) & 31
                keep = (1 - (code >> 23)).astype(F32)
                acc = acc * keep + product(source[slot], ub, ib, day)
                running[place] = acc
            return acc

        if acc is None:
            acc = jnp.zeros((R, TILE), F32)
        return lax.fori_loop(begin // UNROLL, end // UNROLL, visit, acc)

    def each_block(visit, by=4, begin=0, count=BLOCKS):
        def some(step, carry):
            for k in range(by):
                visit(begin + step * by + k)
            return carry

        lax.fori_loop(0, count // by, some, 0)

    def columns(block):
        return pl.ds(pl.multiple_of(block * TILE, TILE), TILE)

    def assemble(order, target, begin=0, count=BLOCKS):
        def visit(block):
            target[block] = running[last[order, block]]

        each_block(visit, 8, begin, count)

    def gram_of(source):
        def four(step, carry):
            total, cross = carry
            for k in range(2):
                block = step * 4 + k * 2
                high, low = halves(jnp.concatenate([source[block], source[block + 1]], axis=1))
                total = total + mm(high, high, NT)
                cross = cross + mm(high, low, NT)
            return total, cross

        zero = jnp.zeros((R, R), F32)
        total, cross = lax.fori_loop(0, BLOCKS // 4, four, (zero, zero))
        return total + (cross + cross.T)

    def fold(gram):
        return jnp.concatenate([gram[: R // 2], gram[R // 2 :]], axis=1)

    def unfold(value):
        return jnp.concatenate([value[:, :R], value[:, R:]], axis=0)

    def squares(source, begin, count):
        total = jnp.zeros((8, TILE), F32)
        for step in range(count):
            value = source[begin + step]
            value = value * value
            total = total + jnp.sum(value.reshape(8, 8, TILE), axis=0)
        return total

    def scale_of(total, entries):
        total = jnp.sum(jnp.sum(total, axis=1, keepdims=True), axis=0, keepdims=True)
        return jnp.sqrt(total / entries + EPSILON)

    def prior_part(inv, prior):
        def visit(step, carry):
            wide = prior[:, pl.ds(pl.multiple_of(step * 4 * TILE, 4 * TILE), 4 * TILE)]
            wide = mm(inv, right_three(wide))
            for k in range(4):
                t2[step * 4 + k] = wide[:, k * TILE : (k + 1) * TILE]
            return carry

        lax.fori_loop(0, BLOCKS // 4, visit, 0)

    def apply(inv, source, begin, count, target):
        for step in range(count):
            target[begin + step] = mm(inv, right_three(source[begin + step]))

    def finish(target, target_half, t1, norm, out=None, begin=0, count=BLOCKS):
        share = 1.0 / norm

        def visit(block):
            value = t1[block] * share + t2[block]
            target[block] = value
            target_half[block] = value.astype(BF16)
            if out is not None:
                out[:, columns(block)] = value

        each_block(visit, 4, begin, count)

    order_slots(index, live_count[0], codes_made, last_made)
    codes_copy = pltpu.make_async_copy(codes_made, codes, order_sem.at[0])
    last_copy = pltpu.make_async_copy(last_made, last, order_sem.at[1])
    codes_copy.start()
    last_copy.start()

    def lay(block):
        value = user_prior[:, columns(block)]
        users[block] = value
        users_half[block] = value.astype(BF16)
        value = item_prior[:, columns(block)]
        items[block] = value
        items_half[block] = value.astype(BF16)

    for copy in prior_copies:
        copy.wait()
    each_block(lay)
    running[CAP] = jnp.zeros((R, TILE), F32)
    gu_part = fold(gram_of(users))
    day_rows = day_prior[...].T
    lanes = lax.broadcasted_iota(jnp.int32, (R, TILE), 1)

    def transpose_tiles(begin, end):
        def visit(step, carry):
            for k in range(16):
                tiles_t[step * 16 + k] = tiles[step * 16 + k].T
            return carry

        lax.fori_loop(begin // 16, end // 16, visit, 0)

    gu_found = []
    gu_job = total_over(("core", "y", "z"), gu_slots.at[0], gu_part, gu_found)

    for turn in range(PASSES):
        final = turn == PASSES - 1

        if turn == 0:
            tile_copy.wait()
            codes_copy.wait()
            last_copy.wait()

        def day_product(tile, ub, ib, day):
            return mm(users_half[ub], tile) * items_half[ib].astype(F32)

        sweep(2, tiles, day_product)

        def day_sums(step, total):
            for k in range(8):
                day = step * 8 + k
                value = jnp.sum(running[last[2, day]], axis=1, keepdims=True)
                total = jnp.where(lanes == day, value, total)
            return total

        moments = lax.fori_loop(0, DAYS // 8, day_sums, jnp.zeros((R, TILE), F32))
        moments = (moments[:16] + pltpu.roll(moments[16:32], 32, 1)) + (
            pltpu.roll(moments[32:48], 64, 1) + pltpu.roll(moments[48:], 96, 1)
        )
        md_found = []
        md_job = total_over(("core", "x", "yz"), md_slots.at[turn], moments, md_found)
        gv_found = []
        if turn == 0:
            gv_part = fold(gram_of(items))
            pl.semaphore_wait(barrier, len(peers))
            next(gu_job)
            next(md_job)
        else:
            next(md_job)
            gv_part = fold(gram_of(items))
        gv_job = total_over(("x",), gv_slots.at[turn], gv_part, gv_found)
        next(gv_job)
        if turn == 0:
            next(gu_job)
        next(md_job)
        if turn == 0:
            transpose_tiles(0, CAP // 2)
            next(gu_job)
            next(md_job)
            transpose_tiles(CAP // 2, CAP)
            drain(gu_job)
            gram_users = unfold(gu_found[0])
        drain(gv_job)
        gram_items = unfold(gv_found[0])
        if turn:
            next(md_job)
        inv = inverse(gram_users * gram_items)
        drain(md_job)
        moments = md_found[0]
        square = moments * moments
        square = jnp.sum(jnp.sum(square, axis=1, keepdims=True), axis=0, keepdims=True)
        norm = jnp.sqrt(square / (R * DAYS) + EPSILON)
        moments = moments / norm
        moments = jnp.concatenate(
            [moments[:, :DAYS]] + [pltpu.roll(moments, TILE - k * 32, 1)[:, :DAYS] for k in (1, 2, 3)], axis=0
        )
        days = mm(inv, right_three(moments + day_rows))
        for day in range(DAYS):
            spread[day] = jnp.broadcast_to(days[:, day : day + 1], (R, TILE))
        if final:
            day_out[...] = days.T

        def user_product(tile, ub, ib, day):
            return mm((items[ib] * spread[day]).astype(BF16), tile)

        sweep(0, tiles_t, user_product)
        assemble(0, mu)
        parts = [reduce_ring(mu, part, urecv.at[turn, part]) for part in range(2)]
        next(parts[0])
        next(parts[0])
        next(parts[1])
        high, low = halves(days)
        cross = mm(high, low, NT)
        gram_days = mm(high, high, NT) + (cross + mm(low, high, NT))
        inv = inverse(gram_items * gram_days)
        next(parts[0])
        next(parts[1])
        next(parts[1])
        jobs = []
        for part in range(2):
            drain(parts[part])
            apply(inv, mu, x * 8 + 4 * part, 4, t1u.at[turn])
            jobs.append(gather_ring(t1u.at[turn], part))
            next(jobs[part])
        scale_found = []
        scale_job = total_over(
            ("core", "yz", "x"), scale_slots.at[turn, 0], squares(mu, x * 8, 8), scale_found
        )
        next(scale_job)
        next(scale_job)
        prior_part(inv, user_prior)
        next(jobs[0])
        next(jobs[1])
        next(scale_job)
        drain(scale_job)
        for job in jobs:
            drain(job)
        norm = scale_of(scale_found[0], USER_ENTRIES)
        finish(users, users_half, t1u.at[turn], norm, user_prior if final else None)
        if final:
            user_copy = pltpu.make_async_copy(user_prior, user_out, out_sem.at[0])
            user_copy.start()

        gu_found = []
        gu_job = total_over(("core", "y", "z"), gu_slots.at[1 + turn], fold(gram_of(users)), gu_found)
        next(gu_job)

        def item_product(tile, ub, ib, day):
            return mm((users[ub] * spread[day]).astype(BF16), tile)

        acc = sweep(1, tiles, item_product, 0, CAP // 2)
        next(gu_job)
        sweep(1, tiles, item_product, CAP // 2, CAP, acc)
        assemble(1, mi, 16 - core * 16, 16)
        job = reduce_plane(mi, irecv_core.at[turn], irecv.at[turn])
        next(job)
        assemble(1, mi, core * 16, 16)
        next(job)
        drain(gu_job)
        gram_users = unfold(gu_found[0])
        inv = inverse(gram_users * gram_days)
        drain(job)
        scale_found = []
        scale_job = total_over(
            ("yz", "core", "x"), scale_slots.at[turn, 1], squares(mi, core * 16 + plane, 1), scale_found
        )
        next(scale_job)
        apply(inv, mi, core * 16 + plane, 1, t1i.at[turn])
        job = gather_plane(t1i.at[turn])
        next(job)
        prior_part(inv, item_prior)
        next(scale_job)
        next(scale_job)
        next(job)
        drain(scale_job)
        norm = scale_of(scale_found[0], ITEM_ENTRIES)
        out = item_prior if final else None
        item_copies = []
        for part, begin in enumerate((core * 16, 16 - core * 16)):
            if part == 1:
                drain(job)
            finish(items, items_half, t1i.at[turn], norm, out, begin, 16)
            if final:
                half = pl.ds(pl.multiple_of(begin * TILE, 16 * TILE), 16 * TILE)
                copy = pltpu.make_async_copy(item_prior.at[:, half], item_out.at[:, half], out_sem.at[1 + part])
                copy.start()
                item_copies.append(copy)

    user_copy.wait()
    for copy in item_copies:
        copy.wait()


def copy_kernel(user_in, item_in, day_in, user_out, item_out, day_out, sem):
    flying = [
        pltpu.make_async_copy(source, target, sem.at[k])
        for k, (source, target) in enumerate(((user_in, user_out), (item_in, item_out), (day_in, day_out)))
    ]
    for copy in flying:
        copy.start()
    for copy in flying:
        copy.wait()


def copied(arrays):
    return pl.pallas_call(
        copy_kernel,
        out_shape=tuple(jax.ShapeDtypeStruct(one.shape, one.dtype) for one in arrays),
        in_specs=[pl.BlockSpec(memory_space=pltpu.VMEM)] * 3,
        out_specs=(pl.BlockSpec(memory_space=pl.ANY),) * 3,
        scratch_shapes=[pltpu.SemaphoreType.DMA((3,))],
    )(*arrays)


def shards(tile_values, tile_index, tile_count, user_prev, item_prev, day_prior):
    vmem = pl.BlockSpec(memory_space=pltpu.VMEM)
    smem = pl.BlockSpec(memory_space=pltpu.SMEM)
    anywhere = pl.BlockSpec(memory_space=pl.ANY)
    block = (BLOCKS, R, TILE)
    results = pl.pallas_call(
        kernel,
        out_shape=(
            jax.ShapeDtypeStruct(user_prev.shape, F32),
            jax.ShapeDtypeStruct(item_prev.shape, F32),
            jax.ShapeDtypeStruct(day_prior.shape[::-1], F32),
        ),
        in_specs=[vmem, smem, anywhere, anywhere, anywhere, vmem],
        out_specs=(anywhere, anywhere, vmem),
        scratch_shapes=[
            pltpu.VMEM(user_prev.shape, F32),
            pltpu.VMEM(item_prev.shape, F32),
            pltpu.VMEM((CAP, TILE, TILE), BF16),
            pltpu.VMEM((CAP, TILE, TILE), BF16),
            pltpu.VMEM((CAP + 1, R, TILE), F32),
            pltpu.VMEM(block, F32),
            pltpu.VMEM(block, F32),
            pltpu.VMEM(block, BF16),
            pltpu.VMEM(block, BF16),
            pltpu.VMEM(block, F32),
            pltpu.VMEM(block, F32),
            pltpu.VMEM(block, F32),
            pltpu.VMEM((PASSES, *block), F32),
            pltpu.VMEM((PASSES, *block), F32),
            pltpu.VMEM(block, F32),
            pltpu.VMEM((1 + PASSES, 10, R // 2, 2 * R), F32),
            pltpu.VMEM((PASSES, 4, R // 2, 2 * R), F32),
            pltpu.VMEM((PASSES, 22, 16, TILE), F32),
            pltpu.VMEM((PASSES, 2, 22, 8, TILE), F32),
            pltpu.VMEM((PASSES, 2, 6, 2, R, TILE), F32),
            pltpu.VMEM((PASSES, 16, R, TILE), F32),
            pltpu.VMEM((PASSES, 15, R, TILE), F32),
            pltpu.VMEM((8, CAP), jnp.int32),
            pltpu.VMEM((8, TILE), jnp.int32),
            pltpu.SMEM((8, CAP), jnp.int32),
            pltpu.SMEM((8, TILE), jnp.int32),
            pltpu.SemaphoreType.DMA,
            pltpu.SemaphoreType.DMA((2,)),
            pltpu.SemaphoreType.DMA((3,)),
            pltpu.SemaphoreType.DMA((2,)),
            pltpu.SemaphoreType.DMA((GROUPS,)),
            pltpu.SemaphoreType.DMA((GROUPS,)),
        ],
        compiler_params=pltpu.CompilerParams(
            collective_id=0, has_side_effects=True, vmem_limit_bytes=63 * 1024 * 1024
        ),
    )(tile_index, tile_count, tile_values, user_prev, item_prev, day_prior.T)
    users, items, days = copied(results)
    return users, items, days.T


def solution(mesh):
    return jax.shard_map(
        shards,
        mesh=mesh,
        in_specs=(
            P(("au", "ia"), None, None),
            P(None, ("au", "ia")),
            P(("au", "ia")),
            P(None, "au"),
            P(None, "ia"),
            P(),
        ),
        out_specs=(P(None, "au"), P(None, "ia"), P()),
        check_vma=False,
    )
```

```python
import functools

import jax
import jax.numpy as jnp
from jax import lax
from jax.experimental import pallas as pl
from jax.experimental.pallas import tpu as pltpu
from jax.sharding import PartitionSpec as P

PASSES = 2
R = 64
TILE = 128
DAYS = 32
BLOCKS = 32
CAP = 256
EPSILON = 1e-06
USER_ENTRIES = 64 * 131072
ITEM_ENTRIES = 64 * 16384
UNROLL = 64
MESH = pl.DeviceIdType.MESH
F32 = jnp.float32
BF16 = jnp.bfloat16

NN = (((1,), (0,)), ((), ()))
NT = (((1,), (1,)), ((), ()))


def mm(left, right, dims=NN):
    return lax.dot_general(left, right, dims, preferred_element_type=F32)


def halves(values):
    high = values.astype(BF16)
    return high, (values - high.astype(F32)).astype(BF16)


def left_three(values):
    high, low = halves(values)
    return jnp.concatenate([high, high, low], axis=1)


def right_three(values):
    high, low = halves(values)
    return jnp.concatenate([high, low, high], axis=0)


def drain(job):
    for _ in job:
        pass


class Group:
    def __init__(self, sems):
        self.send, self.recv = sems

    def start(self, source, target, device):
        pltpu.make_async_remote_copy(
            src_ref=source,
            dst_ref=target,
            send_sem=self.send,
            recv_sem=self.recv,
            device_id=device,
            device_id_type=MESH,
        ).start()

    def wait(self, all_of_it):
        pltpu.make_async_copy(all_of_it, all_of_it, self.recv).wait()
        pltpu.make_async_copy(all_of_it, all_of_it, self.send).wait()


class Groups:
    def __init__(self, send, recv):
        self.send, self.recv, self.used = send, recv, 0

    def new(self):
        self.used += 1
        return Group((self.send.at[self.used - 1], self.recv.at[self.used - 1]))


GROUPS = 2 + PASSES * (3 + 1 + 3 + 3 + 3 + 4 + 4 + 4 + 1 + 4 + 1)


def order_slots(index, live, codes, last):
    slot = lax.broadcasted_iota(jnp.int32, (8, CAP), 1)
    rows = jnp.concatenate([index[...], jnp.zeros((5, CAP), jnp.int32)], axis=0)
    keys = jnp.where(slot < live, rows, BLOCKS)
    unique = keys * CAP + slot
    unique_down = unique.T
    code = slot[:1] + rows[:1] * 256 + rows[1:2] * 8192 + rows[2:3] * 262144
    ranks = [
        jnp.sum(jnp.where(unique_down[:, k : k + 1] < unique[k : k + 1], 1, 0), axis=0, keepdims=True)
        for k in range(3)
    ]
    down = jnp.concatenate(ranks + [code, slot[:4]], axis=0).T
    keys_down = keys.T
    place = lax.broadcasted_iota(jnp.int32, (CAP, CAP), 1)
    block = lax.broadcasted_iota(jnp.int32, (CAP, TILE), 1)
    for k in range(3):
        chosen = jnp.where(down[:, k : k + 1] == place, down[:, 3:4], 0)
        chosen = jnp.sum(chosen, axis=0, keepdims=True)
        key = jnp.where(slot[:1] < live, (chosen >> (8 + 5 * k)) & 31, BLOCKS)
        starts = (slot[:1] == 0) | (key != pltpu.roll(key, 1, 1))
        codes[k : k + 1, :] = chosen + jnp.where(starts, 1 << 23, 0)
        upto = jnp.sum(jnp.where(keys_down[:, k : k + 1] <= block, 1, 0), axis=0, keepdims=True)
        count = jnp.sum(jnp.where(keys_down[:, k : k + 1] == block, 1, 0), axis=0, keepdims=True)
        last[k : k + 1, :] = jnp.where(count > 0, upto - 1, CAP)


def kernel(
    index, live_count, tiles_hbm, user_hbm, item_hbm, day_prior,
    user_out, item_out, day_out,
    user_prior, item_prior,
    tiles, tiles_t, running, users, items, users_half, items_half, spread,
    mu, mi, t1u, t1i, t2,
    gu_slots, gv_slots, md_slots, scale_slots, urecv, irecv_core, irecv,
    codes_made, last_made, codes, last,
    tile_sem, prior_sem, out_sem, order_sem, send, recv,
):
    au = lax.axis_index("au")
    x = lax.axis_index("ia")
    core = lax.rem(au, 2)
    z = lax.rem(lax.div(au, 2), 4)
    y = lax.div(au, 8)
    plane = y * 4 + z

    def at(yy, zz, cc):
        return (yy * 4 + zz) * 2 + cc

    twin = (at(y, z, 1 - core), x)

    def along_x(step):
        return (au, lax.rem(x + step, 4))

    def along_y(step):
        return (at(lax.rem(y + step, 4), z, core), x)

    def along_z(step):
        return (at(y, lax.rem(z + step, 4), core), x)

    far_first = (2, 1, 3, 0)

    def along_yz(step):
        yy, zz = lax.rem(y + step // 4, 4), lax.rem(z + step % 4, 4)
        return (at(yy, zz, core), x)

    def plane_of(step):
        return lax.rem(y + step // 4, 4) * 4 + lax.rem(z + step % 4, 4)

    kinds = {
        "core": (2, core, lambda step: twin),
        "x": (4, x, along_x),
        "y": (4, y, along_y),
        "z": (4, z, along_z),
        "yz": (16, plane, along_yz),
    }

    def distance(step):
        return (0, 1, 2, 1)[step // 4] + (0, 1, 2, 1)[step % 4]

    orders = {
        2: (1,),
        4: (2, 1, 3),
        16: sorted(range(1, 16), key=lambda step: -distance(step)),
    }

    groups = Groups(send, recv)

    tile_copy = pltpu.make_async_copy(tiles_hbm, tiles, tile_sem)
    prior_copies = [
        pltpu.make_async_copy(user_hbm, user_prior, prior_sem.at[0]),
        pltpu.make_async_copy(item_hbm, item_prior, prior_sem.at[1]),
    ]
    for copy in prior_copies:
        copy.start()
    tile_copy.start()

    barrier = pltpu.get_barrier_semaphore()
    peers = [twin] + [along_x(step) for step in (1, 2, 3)] + [along_yz(step) for step in range(1, 16)]
    for peer in peers:
        pl.semaphore_signal(barrier, inc=1, device_id=peer, device_id_type=MESH)

    def total_over(stages, where, value, result):
        base = 0
        for stage in stages:
            size, mine, along = kinds[stage]
            here = where.at[base + mine]
            where[base + mine] = value
            group = groups.new()
            for step in orders[size]:
                group.start(here, here, along(step))
            yield
            group.wait(where.at[pl.ds(base, size - 1)])
            terms = [where[base + place] for place in range(size)]
            while len(terms) > 1:
                terms = [terms[k] + terms[k + 1] for k in range(0, len(terms), 2)]
            value = terms[0]
            base += size
        result.append(value)

    def ring_part(share, piece):
        return pl.ds(lax.rem(share, 4) * 8 + 2 * piece, 2)

    def reduce_ring(source, part, got):
        first, second = 2 * part, 2 * part + 1
        far, right, left = x + 2, x + 1, x + 3
        distant, close = groups.new(), groups.new()
        distant.start(source.at[ring_part(far, first)], got.at[0], along_x(3))
        distant.start(source.at[ring_part(far, second)], got.at[1], along_x(1))
        yield
        close.start(source.at[ring_part(left, second)], got.at[2], along_x(3))
        close.start(source.at[ring_part(right, first)], got.at[3], along_x(1))
        yield
        distant.wait(got.at[pl.ds(0, 2)])
        here = ring_part(left, first)
        source[here] = source[here] + got[0]
        close.start(source.at[here], got.at[4], along_x(3))
        there = ring_part(right, second)
        source[there] = source[there] + got[1]
        close.start(source.at[there], got.at[5], along_x(1))
        yield
        close.wait(got.at[pl.ds(2, 4)])
        mine = ring_part(x, first)
        source[mine] = source[mine] + (got[4] + got[3])
        mine = ring_part(x, second)
        source[mine] = source[mine] + (got[2] + got[5])

    def gather_ring(source, part):
        def piece(share, which):
            return source.at[ring_part(share, 2 * part + which)]

        left, right = x + 3, x + 1
        onward, rest = groups.new(), groups.new()
        onward.start(piece(x, 0), piece(x, 0), along_x(1))
        onward.start(piece(x, 1), piece(x, 1), along_x(3))
        rest.start(piece(x, 1), piece(x, 1), along_x(1))
        rest.start(piece(x, 0), piece(x, 0), along_x(3))
        yield
        onward.wait(source.at[pl.ds(0, 4)])
        rest.start(piece(left, 0), piece(left, 0), along_x(1))
        rest.start(piece(right, 1), piece(right, 1), along_x(3))
        yield
        rest.wait(source.at[pl.ds(0, 8)])

    def row_of(step):
        return pl.ds(lax.rem(y + step, 4) * 4, 4)

    def reduce_plane(source, got_core, got):
        own, other = core * 16, 16 - core * 16
        between = []
        for row in far_first:
            place = row_of(row)
            group = groups.new()
            group.start(source.at[pl.ds(other + place.start, 4)], got_core.at[place], twin)
            between.append((row, group))
        yield
        flying = groups.new()
        for row, group in between:
            place = row_of(row)
            group.wait(got_core.at[place])
            here = pl.ds(own + place.start, 4)
            source[here] = source[here] + got_core[place]
            for step in (row * 4 + further for further in far_first):
                if step:
                    flying.start(source.at[own + plane_of(step)], got.at[step - 1], along_yz(step))
        yield
        flying.wait(got)
        total = source[own + plane]
        for step in range(15):
            total = total + got[step]
        source[own + plane] = total

    def gather_plane(source):
        own = core * 16
        here = source.at[own + plane]
        flying = {row: groups.new() for row in range(4)}
        for row in far_first:
            for step in (row * 4 + further for further in far_first):
                if step:
                    flying[row].start(here, here, along_yz(step))
        yield
        between = groups.new()
        for row in (0, 1, 3, 2):
            flying[row].wait(source.at[pl.ds(0, 4 if row else 3)])
            place = source.at[pl.ds(own + row_of(4 - row).start, 4)]
            between.start(place, place, twin)
        yield
        between.wait(source.at[pl.ds(0, 16)])

    def inverse(gram):
        rows = lax.broadcasted_iota(jnp.int32, (R, 2 * R), 0)
        lanes = lax.broadcasted_iota(jnp.int32, (R, 2 * R), 1)
        diagonal = jnp.where(rows == lanes, 1.0, 0.0)
        trace = jnp.sum(jnp.sum(gram * diagonal[:, :R], axis=1, keepdims=True), axis=0, keepdims=True)
        matrix = gram / (trace / R) + 0.1 * diagonal[:, :R]
        matrix = jnp.concatenate([matrix, diagonal[:, :R]], axis=1)

        place = rows[:8]

        def wide(column):
            return jnp.broadcast_to(column, (8, 2 * R))

        def eight(_, matrix):
            top = matrix[:8]
            columns = [wide(top[:, k : k + 1]) for k in range(8)]
            for k in range(8):
                share = 1.0 / columns[k][k : k + 1]
                column = (columns[k] - jnp.where(place == k, 1.0, 0.0)) * share
                top = top - column * top[k : k + 1]
                for j in range(k + 1, 8):
                    columns[j] = columns[j] - column * columns[j][k : k + 1]
            rest = []
            for begin in range(8, R, 8):
                value = matrix[begin : begin + 8]
                terms = [wide(value[:, k : k + 1]) * top[k : k + 1] for k in range(8)]
                while len(terms) > 1:
                    terms = [terms[k] + terms[k + 1] for k in range(0, len(terms), 2)]
                rest.append(value - terms[0])
            return pltpu.roll(jnp.concatenate(rest + [top], axis=0), 2 * R - 8, 1)

        return left_three(lax.fori_loop(0, R // 8, eight, matrix)[:, :R])

    def place_of(order, place):
        code = codes[order, place]
        keep = (1 - (code >> 23)).astype(F32)
        return code & 255, (code >> 8) & 31, (code >> 13) & 31, (code >> 18) & 31, keep

    def sweep(order, product, begin=0, end=CAP, acc=None):
        def visit(turn, acc):
            for k in range(UNROLL):
                place = turn * UNROLL + k
                *chosen, keep = place_of(order, place)
                acc = acc * keep + product(place, *chosen)
                running[place] = acc
            return acc

        if acc is None:
            acc = jnp.zeros((R, TILE), F32)
        return lax.fori_loop(begin // UNROLL, end // UNROLL, visit, acc)

    def day_partials(begin, end):
        def visit(turn, carry):
            for k in range(UNROLL):
                place = turn * UNROLL + k
                slot, ub, _, _, _ = place_of(2, place)
                running[place] = mm(users_half[ub], tiles[slot])
            return carry

        lax.fori_loop(begin // UNROLL, end // UNROLL, visit, 0)

    def each_block(visit, by=4, begin=0, count=BLOCKS):
        def some(step, carry):
            for k in range(by):
                visit(begin + step * by + k)
            return carry

        lax.fori_loop(0, count // by, some, 0)

    def columns(block):
        return pl.ds(pl.multiple_of(block * TILE, TILE), TILE)

    def assemble(order, target, begin=0, count=BLOCKS):
        def visit(block):
            target[block] = running[last[order, block]]

        each_block(visit, 8, begin, count)

    def gram_of(source):
        def four(step, carry):
            total, cross = carry
            for k in range(2):
                block = step * 4 + k * 2
                high, low = halves(jnp.concatenate([source[block], source[block + 1]], axis=1))
                total = total + mm(high, high, NT)
                cross = cross + mm(high, low, NT)
            return total, cross

        zero = jnp.zeros((R, R), F32)
        total, cross = lax.fori_loop(0, BLOCKS // 4, four, (zero, zero))
        return total + (cross + cross.T)

    def fold(gram):
        return jnp.concatenate([gram[: R // 2], gram[R // 2 :]], axis=1)

    def unfold(value):
        return jnp.concatenate([value[:, :R], value[:, R:]], axis=0)

    def squares(source, begin, count):
        total = jnp.zeros((8, TILE), F32)
        for step in range(count):
            value = source[begin + step]
            value = value * value
            total = total + jnp.sum(value.reshape(8, 8, TILE), axis=0)
        return total

    def scale_of(total, entries):
        total = jnp.sum(jnp.sum(total, axis=1, keepdims=True), axis=0, keepdims=True)
        return jnp.sqrt(total / entries + EPSILON)

    def prior_part(inv, prior):
        def visit(step, carry):
            wide = prior[:, pl.ds(pl.multiple_of(step * 4 * TILE, 4 * TILE), 4 * TILE)]
            wide = mm(inv, right_three(wide))
            for k in range(4):
                t2[step * 4 + k] = wide[:, k * TILE : (k + 1) * TILE]
            return carry

        lax.fori_loop(0, BLOCKS // 4, visit, 0)

    def apply(inv, source, begin, count, target):
        for step in range(count):
            target[begin + step] = mm(inv, right_three(source[begin + step]))

    def finish(target, target_half, t1, norm, out=None, begin=0, count=BLOCKS):
        share = 1.0 / norm

        def visit(block):
            value = t1[block] * share + t2[block]
            target[block] = value
            target_half[block] = value.astype(BF16)
            if out is not None:
                out[:, columns(block)] = value

        each_block(visit, 4, begin, count)

    order_slots(index, live_count[0], codes_made, last_made)
    codes_copy = pltpu.make_async_copy(codes_made, codes, order_sem.at[0])
    last_copy = pltpu.make_async_copy(last_made, last, order_sem.at[1])
    codes_copy.start()
    last_copy.start()

    def lay(block):
        value = user_prior[:, columns(block)]
        users[block] = value
        users_half[block] = value.astype(BF16)
        value = item_prior[:, columns(block)]
        items[block] = value
        items_half[block] = value.astype(BF16)

    for copy in prior_copies:
        copy.wait()
    each_block(lay)
    running[CAP] = jnp.zeros((R, TILE), F32)
    gu_part = fold(gram_of(users))
    day_rows = day_prior[...].T
    lanes = lax.broadcasted_iota(jnp.int32, (R, TILE), 1)

    def transpose_tiles(begin, end):
        def visit(step, carry):
            for k in range(16):
                tiles_t[step * 16 + k] = tiles[step * 16 + k].T
            return carry

        lax.fori_loop(begin // 16, end // 16, visit, 0)

    gu_found = []
    gu_job = total_over(("core", "yz"), gu_slots.at[0], gu_part, gu_found)

    for turn in range(PASSES):
        final = turn == PASSES - 1

        if turn == 0:
            tile_copy.wait()
            codes_copy.wait()
            last_copy.wait()

        def day_product(place, slot, ub, ib, day):
            if turn == 0:
                return mm(users_half[ub], tiles[slot]) * items_half[ib].astype(F32)
            return running[place] * items_half[ib].astype(F32)

        if turn == 0:
            acc = sweep(2, day_product, 0, CAP // 2)
            pl.semaphore_wait(barrier, len(peers))
            next(gu_job)
            sweep(2, day_product, CAP // 2, CAP, acc)
            next(gu_job)
        else:
            sweep(2, day_product)

        def day_sums(step, total):
            for k in range(8):
                day = step * 8 + k
                value = jnp.sum(running[last[2, day]], axis=1, keepdims=True)
                total = jnp.where(lanes == day, value, total)
            return total

        moments = lax.fori_loop(0, DAYS // 8, day_sums, jnp.zeros((R, TILE), F32))
        moments = (moments[:16] + pltpu.roll(moments[16:32], 32, 1)) + (
            pltpu.roll(moments[32:48], 64, 1) + pltpu.roll(moments[48:], 96, 1)
        )
        md_found = []
        md_job = total_over(("core", "x", "yz"), md_slots.at[turn], moments, md_found)
        next(md_job)
        gv_found = []
        gv_job = total_over(("x",), gv_slots.at[turn], fold(gram_of(items)), gv_found)
        next(gv_job)
        next(md_job)
        if turn == 0:
            transpose_tiles(0, CAP)
            drain(gu_job)
            gram_users = unfold(gu_found[0])
        drain(gv_job)
        gram_items = unfold(gv_found[0])
        next(md_job)
        inv = inverse(gram_users * gram_items)
        ahead = mm(inv, right_three(day_rows))
        drain(md_job)
        moments = md_found[0]
        square = moments * moments
        square = jnp.sum(jnp.sum(square, axis=1, keepdims=True), axis=0, keepdims=True)
        norm = jnp.sqrt(square / (R * DAYS) + EPSILON)
        moments = jnp.concatenate(
            [moments[:, :DAYS]] + [pltpu.roll(moments, TILE - k * 32, 1)[:, :DAYS] for k in (1, 2, 3)], axis=0
        )
        days = mm(inv, right_three(moments)) * (1.0 / norm) + ahead
        for day in range(DAYS):
            spread[day] = jnp.broadcast_to(days[:, day : day + 1], (R, TILE))
        if final:
            day_out[...] = days.T

        def user_product(place, slot, ub, ib, day):
            return mm((items[ib] * spread[day]).astype(BF16), tiles_t[slot])

        sweep(0, user_product)
        assemble(0, mu)
        parts = [reduce_ring(mu, part, urecv.at[turn, part]) for part in range(2)]
        next(parts[0])
        next(parts[0])
        next(parts[1])
        high, low = halves(days)
        cross = mm(high, low, NT)
        gram_days = mm(high, high, NT) + (cross + mm(low, high, NT))
        inv = inverse(gram_items * gram_days)
        next(parts[0])
        next(parts[1])
        next(parts[1])
        jobs = []
        for part in range(2):
            drain(parts[part])
            apply(inv, mu, x * 8 + 4 * part, 4, t1u.at[turn])
            jobs.append(gather_ring(t1u.at[turn], part))
            next(jobs[part])
        scale_found = []
        scale_job = total_over(
            ("core", "yz", "x"), scale_slots.at[turn, 0], squares(mu, x * 8, 8), scale_found
        )
        next(scale_job)
        next(scale_job)
        prior_part(inv, user_prior)
        next(jobs[0])
        next(jobs[1])
        next(scale_job)
        drain(scale_job)
        for job in jobs:
            drain(job)
        norm = scale_of(scale_found[0], USER_ENTRIES)
        finish(users, users_half, t1u.at[turn], norm, user_prior if final else None)
        if final:
            user_copy = pltpu.make_async_copy(user_prior, user_out, out_sem.at[0])
            user_copy.start()

        gu_found = []
        gu_job = total_over(("core", "y", "z"), gu_slots.at[1 + turn], fold(gram_of(users)), gu_found)
        next(gu_job)

        def item_product(place, slot, ub, ib, day):
            return mm((users[ub] * spread[day]).astype(BF16), tiles[slot])

        acc = sweep(1, item_product, 0, CAP // 2)
        next(gu_job)
        sweep(1, item_product, CAP // 2, CAP, acc)
        assemble(1, mi, 16 - core * 16, 16)
        job = reduce_plane(mi, irecv_core.at[turn], irecv.at[turn])
        next(job)
        assemble(1, mi, core * 16, 16)
        next(job)
        if not final:
            day_partials(0, CAP // 2)
        next(gu_job)
        if not final:
            day_partials(CAP // 2, CAP)
        drain(gu_job)
        gram_users = unfold(gu_found[0])
        inv = inverse(gram_users * gram_days)
        drain(job)
        scale_found = []
        scale_job = total_over(
            ("yz", "core", "x"), scale_slots.at[turn, 1], squares(mi, core * 16 + plane, 1), scale_found
        )
        next(scale_job)
        apply(inv, mi, core * 16 + plane, 1, t1i.at[turn])
        job = gather_plane(t1i.at[turn])
        next(job)
        prior_part(inv, item_prior)
        next(scale_job)
        next(scale_job)
        next(job)
        drain(scale_job)
        norm = scale_of(scale_found[0], ITEM_ENTRIES)
        out = item_prior if final else None
        item_copies = []
        for part, begin in enumerate((core * 16, 16 - core * 16)):
            if part == 1:
                drain(job)
            finish(items, items_half, t1i.at[turn], norm, out, begin, 16)
            if final:
                half = pl.ds(pl.multiple_of(begin * TILE, 16 * TILE), 16 * TILE)
                copy = pltpu.make_async_copy(item_prior.at[:, half], item_out.at[:, half], out_sem.at[1 + part])
                copy.start()
                item_copies.append(copy)

    user_copy.wait()
    for copy in item_copies:
        copy.wait()


def copy_kernel(user_in, item_in, day_in, user_out, item_out, day_out, sem):
    flying = [
        pltpu.make_async_copy(source, target, sem.at[k])
        for k, (source, target) in enumerate(((user_in, user_out), (item_in, item_out), (day_in, day_out)))
    ]
    for copy in flying:
        copy.start()
    for copy in flying:
        copy.wait()


def copied(arrays):
    return pl.pallas_call(
        copy_kernel,
        out_shape=tuple(jax.ShapeDtypeStruct(one.shape, one.dtype) for one in arrays),
        in_specs=[pl.BlockSpec(memory_space=pltpu.VMEM)] * 3,
        out_specs=(pl.BlockSpec(memory_space=pl.ANY),) * 3,
        scratch_shapes=[pltpu.SemaphoreType.DMA((3,))],
    )(*arrays)


def shards(tile_values, tile_index, tile_count, user_prev, item_prev, day_prior):
    vmem = pl.BlockSpec(memory_space=pltpu.VMEM)
    smem = pl.BlockSpec(memory_space=pltpu.SMEM)
    anywhere = pl.BlockSpec(memory_space=pl.ANY)
    block = (BLOCKS, R, TILE)
    results = pl.pallas_call(
        kernel,
        out_shape=(
            jax.ShapeDtypeStruct(user_prev.shape, F32),
            jax.ShapeDtypeStruct(item_prev.shape, F32),
            jax.ShapeDtypeStruct(day_prior.shape[::-1], F32),
        ),
        in_specs=[vmem, smem, anywhere, anywhere, anywhere, vmem],
        out_specs=(anywhere, anywhere, vmem),
        scratch_shapes=[
            pltpu.VMEM(user_prev.shape, F32),
            pltpu.VMEM(item_prev.shape, F32),
            pltpu.VMEM((CAP, TILE, TILE), BF16),
            pltpu.VMEM((CAP, TILE, TILE), BF16),
            pltpu.VMEM((CAP + 1, R, TILE), F32),
            pltpu.VMEM(block, F32),
            pltpu.VMEM(block, F32),
            pltpu.VMEM(block, BF16),
            pltpu.VMEM(block, BF16),
            pltpu.VMEM(block, F32),
            pltpu.VMEM(block, F32),
            pltpu.VMEM(block, F32),
            pltpu.VMEM((PASSES, *block), F32),
            pltpu.VMEM((PASSES, *block), F32),
            pltpu.VMEM(block, F32),
            pltpu.VMEM((1 + PASSES, 18, R // 2, 2 * R), F32),
            pltpu.VMEM((PASSES, 4, R // 2, 2 * R), F32),
            pltpu.VMEM((PASSES, 22, 16, TILE), F32),
            pltpu.VMEM((PASSES, 2, 22, 8, TILE), F32),
            pltpu.VMEM((PASSES, 2, 6, 2, R, TILE), F32),
            pltpu.VMEM((PASSES, 16, R, TILE), F32),
            pltpu.VMEM((PASSES, 15, R, TILE), F32),
            pltpu.VMEM((8, CAP), jnp.int32),
            pltpu.VMEM((8, TILE), jnp.int32),
            pltpu.SMEM((8, CAP), jnp.int32),
            pltpu.SMEM((8, TILE), jnp.int32),
            pltpu.SemaphoreType.DMA,
            pltpu.SemaphoreType.DMA((2,)),
            pltpu.SemaphoreType.DMA((3,)),
            pltpu.SemaphoreType.DMA((2,)),
            pltpu.SemaphoreType.DMA((GROUPS,)),
            pltpu.SemaphoreType.DMA((GROUPS,)),
        ],
        compiler_params=pltpu.CompilerParams(
            collective_id=0, has_side_effects=True, vmem_limit_bytes=63 * 1024 * 1024
        ),
    )(tile_index, tile_count, tile_values, user_prev, item_prev, day_prior.T)
    users, items, days = copied(results)
    return users, items, days.T


def solution(mesh):
    return jax.shard_map(
        shards,
        mesh=mesh,
        in_specs=(
            P(("au", "ia"), None, None),
            P(None, ("au", "ia")),
            P(("au", "ia")),
            P(None, "au"),
            P(None, "ia"),
            P(),
        ),
        out_specs=(P(None, "au"), P(None, "ia"), P()),
        check_vma=False,
    )
```

```python
import functools

import jax
import jax.numpy as jnp
from jax import lax
from jax.experimental import pallas as pl
from jax.experimental.pallas import tpu as pltpu
from jax.sharding import PartitionSpec as P

PASSES = 2
R = 64
TILE = 128
DAYS = 32
BLOCKS = 32
CAP = 256
EPSILON = 1e-06
USER_ENTRIES = 64 * 131072
ITEM_ENTRIES = 64 * 16384
UNROLL = 64
MESH = pl.DeviceIdType.MESH
F32 = jnp.float32
BF16 = jnp.bfloat16

NN = (((1,), (0,)), ((), ()))
NT = (((1,), (1,)), ((), ()))


def mm(left, right, dims=NN):
    return lax.dot_general(left, right, dims, preferred_element_type=F32)


def halves(values):
    high = values.astype(BF16)
    return high, (values - high.astype(F32)).astype(BF16)


def left_three(values):
    high, low = halves(values)
    return jnp.concatenate([high, high, low], axis=1)


def right_three(values):
    high, low = halves(values)
    return jnp.concatenate([high, low, high], axis=0)


def drain(job):
    for _ in job:
        pass


class Group:
    def __init__(self, sems):
        self.send, self.recv = sems

    def start(self, source, target, device):
        pltpu.make_async_remote_copy(
            src_ref=source,
            dst_ref=target,
            send_sem=self.send,
            recv_sem=self.recv,
            device_id=device,
            device_id_type=MESH,
        ).start()

    def wait(self, all_of_it):
        pltpu.make_async_copy(all_of_it, all_of_it, self.recv).wait()
        pltpu.make_async_copy(all_of_it, all_of_it, self.send).wait()


class Groups:
    def __init__(self, send, recv):
        self.send, self.recv, self.used = send, recv, 0

    def new(self):
        self.used += 1
        return Group((self.send.at[self.used - 1], self.recv.at[self.used - 1]))


GROUPS = 2 + PASSES * (3 + 1 + 3 + 3 + 3 + 4 + 4 + 4 + 1 + 15 + 1)


def order_slots(index, live, codes, last):
    slot = lax.broadcasted_iota(jnp.int32, (8, CAP), 1)
    rows = jnp.concatenate([index[...], jnp.zeros((5, CAP), jnp.int32)], axis=0)
    keys = jnp.where(slot < live, rows, BLOCKS)
    unique = keys * CAP + slot
    unique_down = unique.T
    code = slot[:1] + rows[:1] * 256 + rows[1:2] * 8192 + rows[2:3] * 262144
    ranks = [
        jnp.sum(jnp.where(unique_down[:, k : k + 1] < unique[k : k + 1], 1, 0), axis=0, keepdims=True)
        for k in range(3)
    ]
    down = jnp.concatenate(ranks + [code, slot[:4]], axis=0).T
    keys_down = keys.T
    place = lax.broadcasted_iota(jnp.int32, (CAP, CAP), 1)
    block = lax.broadcasted_iota(jnp.int32, (CAP, TILE), 1)
    for k in range(3):
        chosen = jnp.where(down[:, k : k + 1] == place, down[:, 3:4], 0)
        chosen = jnp.sum(chosen, axis=0, keepdims=True)
        key = jnp.where(slot[:1] < live, (chosen >> (8 + 5 * k)) & 31, BLOCKS)
        starts = (slot[:1] == 0) | (key != pltpu.roll(key, 1, 1))
        codes[k : k + 1, :] = chosen + jnp.where(starts, 1 << 23, 0)
        upto = jnp.sum(jnp.where(keys_down[:, k : k + 1] <= block, 1, 0), axis=0, keepdims=True)
        count = jnp.sum(jnp.where(keys_down[:, k : k + 1] == block, 1, 0), axis=0, keepdims=True)
        last[k : k + 1, :] = jnp.where(count > 0, upto - 1, CAP)


def kernel(
    index, live_count, tiles_hbm, user_hbm, item_hbm, day_prior,
    user_out, item_out, day_out,
    user_prior, item_prior,
    tiles, tiles_t, running, users, items, users_half, items_half, spread,
    mu, mi, t1u, t1i, t2,
    gu_slots, gv_slots, md_slots, scale_slots, urecv, irecv_core, irecv,
    codes_made, last_made, codes, last,
    tile_sem, prior_sem, out_sem, order_sem, send, recv,
):
    au = lax.axis_index("au")
    x = lax.axis_index("ia")
    core = lax.rem(au, 2)
    z = lax.rem(lax.div(au, 2), 4)
    y = lax.div(au, 8)
    plane = y * 4 + z

    def at(yy, zz, cc):
        return (yy * 4 + zz) * 2 + cc

    twin = (at(y, z, 1 - core), x)

    def along_x(step):
        return (au, lax.rem(x + step, 4))

    def along_y(step):
        return (at(lax.rem(y + step, 4), z, core), x)

    def along_z(step):
        return (at(y, lax.rem(z + step, 4), core), x)

    far_first = (2, 1, 3, 0)

    def along_yz(step):
        yy, zz = lax.rem(y + step // 4, 4), lax.rem(z + step % 4, 4)
        return (at(yy, zz, core), x)

    def plane_of(step):
        return lax.rem(y + step // 4, 4) * 4 + lax.rem(z + step % 4, 4)

    kinds = {
        "core": (2, core, lambda step: twin),
        "x": (4, x, along_x),
        "y": (4, y, along_y),
        "z": (4, z, along_z),
        "yz": (16, plane, along_yz),
    }

    def distance(step):
        return (0, 1, 2, 1)[step // 4] + (0, 1, 2, 1)[step % 4]

    orders = {
        2: (1,),
        4: (2, 1, 3),
        16: sorted(range(1, 16), key=lambda step: -distance(step)),
    }

    groups = Groups(send, recv)

    tile_copy = pltpu.make_async_copy(tiles_hbm, tiles, tile_sem)
    prior_copies = [
        pltpu.make_async_copy(user_hbm, user_prior, prior_sem.at[0]),
        pltpu.make_async_copy(item_hbm, item_prior, prior_sem.at[1]),
    ]
    for copy in prior_copies:
        copy.start()
    tile_copy.start()

    barrier = pltpu.get_barrier_semaphore()
    peers = [twin] + [along_x(step) for step in (1, 2, 3)] + [along_yz(step) for step in range(1, 16)]
    for peer in peers:
        pl.semaphore_signal(barrier, inc=1, device_id=peer, device_id_type=MESH)

    def total_over(stages, where, value, result):
        base = 0
        for stage in stages:
            size, mine, along = kinds[stage]
            here = where.at[base + mine]
            where[base + mine] = value
            group = groups.new()
            for step in orders[size]:
                group.start(here, here, along(step))
            yield
            group.wait(where.at[pl.ds(base, size - 1)])
            terms = [where[base + place] for place in range(size)]
            while len(terms) > 1:
                terms = [terms[k] + terms[k + 1] for k in range(0, len(terms), 2)]
            value = terms[0]
            base += size
        result.append(value)

    def ring_part(share, piece):
        return pl.ds(lax.rem(share, 4) * 8 + 2 * piece, 2)

    def reduce_ring(source, part, got):
        first, second = 2 * part, 2 * part + 1
        far, right, left = x + 2, x + 1, x + 3
        distant, close = groups.new(), groups.new()
        distant.start(source.at[ring_part(far, first)], got.at[0], along_x(3))
        distant.start(source.at[ring_part(far, second)], got.at[1], along_x(1))
        yield
        close.start(source.at[ring_part(left, second)], got.at[2], along_x(3))
        close.start(source.at[ring_part(right, first)], got.at[3], along_x(1))
        yield
        distant.wait(got.at[pl.ds(0, 2)])
        here = ring_part(left, first)
        source[here] = source[here] + got[0]
        close.start(source.at[here], got.at[4], along_x(3))
        there = ring_part(right, second)
        source[there] = source[there] + got[1]
        close.start(source.at[there], got.at[5], along_x(1))
        yield
        close.wait(got.at[pl.ds(2, 4)])
        mine = ring_part(x, first)
        source[mine] = source[mine] + (got[4] + got[3])
        mine = ring_part(x, second)
        source[mine] = source[mine] + (got[2] + got[5])

    def gather_ring(source, part):
        def piece(share, which):
            return source.at[ring_part(share, 2 * part + which)]

        left, right = x + 3, x + 1
        onward, rest = groups.new(), groups.new()
        onward.start(piece(x, 0), piece(x, 0), along_x(1))
        onward.start(piece(x, 1), piece(x, 1), along_x(3))
        rest.start(piece(x, 1), piece(x, 1), along_x(1))
        rest.start(piece(x, 0), piece(x, 0), along_x(3))
        yield
        onward.wait(source.at[pl.ds(0, 4)])
        rest.start(piece(left, 0), piece(left, 0), along_x(1))
        rest.start(piece(right, 1), piece(right, 1), along_x(3))
        yield
        rest.wait(source.at[pl.ds(0, 8)])

    def row_of(step):
        return pl.ds(lax.rem(y + step, 4) * 4, 4)

    def reduce_plane(source, got_core, got):
        own, other = core * 16, 16 - core * 16
        between = []
        for row in far_first:
            place = row_of(row)
            group = groups.new()
            group.start(source.at[pl.ds(other + place.start, 4)], got_core.at[place], twin)
            between.append((row, group))
        yield
        flying = groups.new()
        for row, group in between:
            place = row_of(row)
            group.wait(got_core.at[place])
            here = pl.ds(own + place.start, 4)
            source[here] = source[here] + got_core[place]
            for step in (row * 4 + further for further in far_first):
                if step:
                    flying.start(source.at[own + plane_of(step)], got.at[step - 1], along_yz(step))
        yield
        flying.wait(got)
        total = source[own + plane]
        for step in range(15):
            total = total + got[step]
        source[own + plane] = total

    def gather_plane(source):
        own = core * 16
        here = source.at[own + plane]
        flying = {step: groups.new() for step in orders[16]}
        for step in orders[16]:
            flying[step].start(here, here, along_yz(step))
        yield
        between = groups.new()
        between.start(here, here, twin)
        for step in reversed(orders[16]):
            back = (4 - step // 4) % 4 * 4 + (4 - step % 4) % 4
            place = source.at[own + plane_of(back)]
            flying[step].wait(place)
            between.start(place, place, twin)
        yield
        between.wait(source.at[pl.ds(0, 16)])

    def inverse(gram):
        rows = lax.broadcasted_iota(jnp.int32, (R, 2 * R), 0)
        lanes = lax.broadcasted_iota(jnp.int32, (R, 2 * R), 1)
        diagonal = jnp.where(rows == lanes, 1.0, 0.0)
        trace = jnp.sum(jnp.sum(gram * diagonal[:, :R], axis=1, keepdims=True), axis=0, keepdims=True)
        matrix = gram / (trace / R) + 0.1 * diagonal[:, :R]
        matrix = jnp.concatenate([matrix, diagonal[:, :R]], axis=1)

        place = rows[:8]

        def wide(column):
            return jnp.broadcast_to(column, (8, 2 * R))

        def eight(_, matrix):
            top = matrix[:8]
            columns = [wide(top[:, k : k + 1]) for k in range(8)]
            for k in range(8):
                share = 1.0 / columns[k][k : k + 1]
                column = (columns[k] - jnp.where(place == k, 1.0, 0.0)) * share
                top = top - column * top[k : k + 1]
                for j in range(k + 1, 8):
                    columns[j] = columns[j] - column * columns[j][k : k + 1]
            rest = []
            for begin in range(8, R, 8):
                value = matrix[begin : begin + 8]
                terms = [wide(value[:, k : k + 1]) * top[k : k + 1] for k in range(8)]
                while len(terms) > 1:
                    terms = [terms[k] + terms[k + 1] for k in range(0, len(terms), 2)]
                rest.append(value - terms[0])
            return pltpu.roll(jnp.concatenate(rest + [top], axis=0), 2 * R - 8, 1)

        return left_three(lax.fori_loop(0, R // 8, eight, matrix)[:, :R])

    def place_of(order, place):
        code = codes[order, place]
        keep = (1 - (code >> 23)).astype(F32)
        return code & 255, (code >> 8) & 31, (code >> 13) & 31, (code >> 18) & 31, keep

    def sweep(order, product, begin=0, end=CAP, acc=None):
        def visit(turn, acc):
            for k in range(UNROLL):
                place = turn * UNROLL + k
                *chosen, keep = place_of(order, place)
                acc = acc * keep + product(place, *chosen)
                running[place] = acc
            return acc

        if acc is None:
            acc = jnp.zeros((R, TILE), F32)
        return lax.fori_loop(begin // UNROLL, end // UNROLL, visit, acc)

    def day_partials(begin, end):
        def visit(turn, carry):
            for k in range(UNROLL):
                place = turn * UNROLL + k
                slot, ub, _, _, _ = place_of(2, place)
                running[place] = mm(users_half[ub], tiles[slot])
            return carry

        lax.fori_loop(begin // UNROLL, end // UNROLL, visit, 0)

    def each_block(visit, by=4, begin=0, count=BLOCKS):
        def some(step, carry):
            for k in range(by):
                visit(begin + step * by + k)
            return carry

        lax.fori_loop(0, count // by, some, 0)

    def columns(block):
        return pl.ds(pl.multiple_of(block * TILE, TILE), TILE)

    def assemble(order, target, begin=0, count=BLOCKS):
        def visit(block):
            target[block] = running[last[order, block]]

        each_block(visit, 8, begin, count)

    def gram_of(source):
        def eight(step, carry):
            total, cross = carry
            for k in range(4):
                block = step * 8 + k * 2
                high, low = halves(jnp.concatenate([source[block], source[block + 1]], axis=1))
                total = total + mm(high, high, NT)
                cross = cross + mm(high, low, NT)
            return total, cross

        zero = jnp.zeros((R, R), F32)
        total, cross = lax.fori_loop(0, BLOCKS // 8, eight, (zero, zero))
        return total + (cross + cross.T)

    def fold(gram):
        return jnp.concatenate([gram[: R // 2], gram[R // 2 :]], axis=1)

    def unfold(value):
        return jnp.concatenate([value[:, :R], value[:, R:]], axis=0)

    def squares(source, begin, count):
        total = jnp.zeros((8, TILE), F32)
        for step in range(count):
            value = source[begin + step]
            value = value * value
            total = total + jnp.sum(value.reshape(8, 8, TILE), axis=0)
        return total

    def scale_of(total, entries):
        total = jnp.sum(jnp.sum(total, axis=1, keepdims=True), axis=0, keepdims=True)
        return jnp.sqrt(total / entries + EPSILON)

    def prior_part(inv, prior):
        def visit(step, carry):
            wide = prior[:, pl.ds(pl.multiple_of(step * 4 * TILE, 4 * TILE), 4 * TILE)]
            wide = mm(inv, right_three(wide))
            for k in range(4):
                t2[step * 4 + k] = wide[:, k * TILE : (k + 1) * TILE]
            return carry

        lax.fori_loop(0, BLOCKS // 4, visit, 0)

    def apply(inv, source, begin, count, target):
        for step in range(count):
            target[begin + step] = mm(inv, right_three(source[begin + step]))

    def finish(target, target_half, t1, norm, out=None, begin=0, count=BLOCKS):
        share = 1.0 / norm

        def visit(block):
            value = t1[block] * share + t2[block]
            target[block] = value
            target_half[block] = value.astype(BF16)
            if out is not None:
                out[:, columns(block)] = value

        each_block(visit, 8, begin, count)

    order_slots(index, live_count[0], codes_made, last_made)
    codes_copy = pltpu.make_async_copy(codes_made, codes, order_sem.at[0])
    last_copy = pltpu.make_async_copy(last_made, last, order_sem.at[1])
    codes_copy.start()
    last_copy.start()

    def lay(block):
        value = user_prior[:, columns(block)]
        users[block] = value
        users_half[block] = value.astype(BF16)
        value = item_prior[:, columns(block)]
        items[block] = value
        items_half[block] = value.astype(BF16)

    for copy in prior_copies:
        copy.wait()
    each_block(lay)
    running[CAP] = jnp.zeros((R, TILE), F32)
    gu_part = fold(gram_of(users))
    day_rows = day_prior[...].T
    lanes = lax.broadcasted_iota(jnp.int32, (R, TILE), 1)

    def transpose_tiles(begin, end):
        def visit(step, carry):
            for k in range(16):
                tiles_t[step * 16 + k] = tiles[step * 16 + k].T
            return carry

        lax.fori_loop(begin // 16, end // 16, visit, 0)

    gu_found = []
    gu_job = total_over(("core", "yz"), gu_slots.at[0], gu_part, gu_found)

    for turn in range(PASSES):
        final = turn == PASSES - 1

        if turn == 0:
            tile_copy.wait()
            codes_copy.wait()
            last_copy.wait()

        def day_product(place, slot, ub, ib, day):
            if turn == 0:
                return mm(users_half[ub], tiles[slot]) * items_half[ib].astype(F32)
            return running[place] * items_half[ib].astype(F32)

        if turn == 0:
            acc = sweep(2, day_product, 0, CAP // 2)
            pl.semaphore_wait(barrier, len(peers))
            next(gu_job)
            sweep(2, day_product, CAP // 2, CAP, acc)
            next(gu_job)
        else:
            sweep(2, day_product)

        def day_sums(step, total):
            for k in range(16):
                day = step * 16 + k
                value = jnp.sum(running[last[2, day]], axis=1, keepdims=True)
                total = jnp.where(lanes == day, value, total)
            return total

        moments = lax.fori_loop(0, DAYS // 16, day_sums, jnp.zeros((R, TILE), F32))
        moments = (moments[:16] + pltpu.roll(moments[16:32], 32, 1)) + (
            pltpu.roll(moments[32:48], 64, 1) + pltpu.roll(moments[48:], 96, 1)
        )
        md_found = []
        md_job = total_over(("core", "x", "yz"), md_slots.at[turn], moments, md_found)
        next(md_job)
        gv_found = []
        gv_job = total_over(("x",), gv_slots.at[turn], fold(gram_of(items)), gv_found)
        next(gv_job)
        next(md_job)
        if turn == 0:
            transpose_tiles(0, CAP)
            drain(gu_job)
            gram_users = unfold(gu_found[0])
        drain(gv_job)
        gram_items = unfold(gv_found[0])
        next(md_job)
        inv = inverse(gram_users * gram_items)
        ahead = mm(inv, right_three(day_rows))
        drain(md_job)
        moments = md_found[0]
        square = moments * moments
        square = jnp.sum(jnp.sum(square, axis=1, keepdims=True), axis=0, keepdims=True)
        norm = jnp.sqrt(square / (R * DAYS) + EPSILON)
        moments = jnp.concatenate(
            [moments[:, :DAYS]] + [pltpu.roll(moments, TILE - k * 32, 1)[:, :DAYS] for k in (1, 2, 3)], axis=0
        )
        days = mm(inv, right_three(moments)) * (1.0 / norm) + ahead
        for day in range(DAYS):
            spread[day] = jnp.broadcast_to(days[:, day : day + 1], (R, TILE))
        if final:
            day_out[...] = days.T

        def user_product(place, slot, ub, ib, day):
            return mm((items[ib] * spread[day]).astype(BF16), tiles_t[slot])

        sweep(0, user_product)
        assemble(0, mu)
        parts = [reduce_ring(mu, part, urecv.at[turn, part]) for part in range(2)]
        next(parts[0])
        next(parts[0])
        next(parts[1])
        high, low = halves(days)
        cross = mm(high, low, NT)
        gram_days = mm(high, high, NT) + (cross + mm(low, high, NT))
        inv = inverse(gram_items * gram_days)
        next(parts[0])
        next(parts[1])
        next(parts[1])
        jobs = []
        for part in range(2):
            drain(parts[part])
            apply(inv, mu, x * 8 + 4 * part, 4, t1u.at[turn])
            jobs.append(gather_ring(t1u.at[turn], part))
            next(jobs[part])
        scale_found = []
        scale_job = total_over(
            ("core", "yz", "x"), scale_slots.at[turn, 0], squares(mu, x * 8, 8), scale_found
        )
        next(scale_job)
        next(scale_job)
        prior_part(inv, user_prior)
        next(jobs[0])
        next(jobs[1])
        next(scale_job)
        drain(scale_job)
        for job in jobs:
            drain(job)
        norm = scale_of(scale_found[0], USER_ENTRIES)
        finish(users, users_half, t1u.at[turn], norm, user_prior if final else None)
        if final:
            user_copy = pltpu.make_async_copy(user_prior, user_out, out_sem.at[0])
            user_copy.start()

        gu_found = []
        gu_job = total_over(("core", "y", "z"), gu_slots.at[1 + turn], fold(gram_of(users)), gu_found)
        next(gu_job)

        def item_product(place, slot, ub, ib, day):
            return mm((users[ub] * spread[day]).astype(BF16), tiles[slot])

        acc = sweep(1, item_product, 0, CAP // 2)
        next(gu_job)
        sweep(1, item_product, CAP // 2, CAP, acc)
        assemble(1, mi, 16 - core * 16, 16)
        job = reduce_plane(mi, irecv_core.at[turn], irecv.at[turn])
        next(job)
        assemble(1, mi, core * 16, 16)
        next(job)
        if not final:
            day_partials(0, CAP // 2)
        next(gu_job)
        if not final:
            day_partials(CAP // 2, CAP)
        drain(gu_job)
        gram_users = unfold(gu_found[0])
        inv = inverse(gram_users * gram_days)
        drain(job)
        scale_found = []
        scale_job = total_over(
            ("yz", "core", "x"), scale_slots.at[turn, 1], squares(mi, core * 16 + plane, 1), scale_found
        )
        next(scale_job)
        apply(inv, mi, core * 16 + plane, 1, t1i.at[turn])
        job = gather_plane(t1i.at[turn])
        next(job)
        prior_part(inv, item_prior)
        next(scale_job)
        next(scale_job)
        next(job)
        drain(scale_job)
        norm = scale_of(scale_found[0], ITEM_ENTRIES)
        out = item_prior if final else None
        item_copies = []
        for part, begin in enumerate((core * 16, 16 - core * 16)):
            if part == 1:
                drain(job)
            finish(items, items_half, t1i.at[turn], norm, out, begin, 16)
            if final:
                half = pl.ds(pl.multiple_of(begin * TILE, 16 * TILE), 16 * TILE)
                copy = pltpu.make_async_copy(item_prior.at[:, half], item_out.at[:, half], out_sem.at[1 + part])
                copy.start()
                item_copies.append(copy)

    user_copy.wait()
    for copy in item_copies:
        copy.wait()


PIECES = 4


def copy_kernel(user_in, item_in, day_in, user_out, item_out, day_out, user_held, item_held, day_held, sem):
    jobs = [(day_in, day_held, day_out)]
    for source, held, target in ((user_in, user_held, user_out), (item_in, item_held, item_out)):
        size = R // PIECES
        for k in range(PIECES):
            rows = pl.ds(k * size, size)
            jobs.append((source.at[rows], held.at[rows], target.at[rows]))
    arriving = [pltpu.make_async_copy(one[0], one[1], sem.at[0, k]) for k, one in enumerate(jobs)]
    leaving = [pltpu.make_async_copy(one[1], one[2], sem.at[1, k]) for k, one in enumerate(jobs)]
    for copy in arriving:
        copy.start()
    for copy, onward in zip(arriving, leaving):
        copy.wait()
        onward.start()
    for copy in leaving:
        copy.wait()


def copied(arrays):
    anywhere = pl.BlockSpec(memory_space=pl.ANY)
    return pl.pallas_call(
        copy_kernel,
        out_shape=tuple(jax.ShapeDtypeStruct(one.shape, one.dtype) for one in arrays),
        in_specs=[anywhere] * 3,
        out_specs=(anywhere,) * 3,
        scratch_shapes=[pltpu.VMEM(one.shape, one.dtype) for one in arrays]
        + [pltpu.SemaphoreType.DMA((2, 1 + 2 * PIECES))],
        compiler_params=pltpu.CompilerParams(vmem_limit_bytes=63 * 1024 * 1024),
    )(*arrays)


def shards(tile_values, tile_index, tile_count, user_prev, item_prev, day_prior):
    vmem = pl.BlockSpec(memory_space=pltpu.VMEM)
    smem = pl.BlockSpec(memory_space=pltpu.SMEM)
    anywhere = pl.BlockSpec(memory_space=pl.ANY)
    block = (BLOCKS, R, TILE)
    results = pl.pallas_call(
        kernel,
        out_shape=(
            jax.ShapeDtypeStruct(user_prev.shape, F32),
            jax.ShapeDtypeStruct(item_prev.shape, F32),
            jax.ShapeDtypeStruct(day_prior.shape[::-1], F32),
        ),
        in_specs=[vmem, smem, anywhere, anywhere, anywhere, vmem],
        out_specs=(anywhere, anywhere, vmem),
        scratch_shapes=[
            pltpu.VMEM(user_prev.shape, F32),
            pltpu.VMEM(item_prev.shape, F32),
            pltpu.VMEM((CAP, TILE, TILE), BF16),
            pltpu.VMEM((CAP, TILE, TILE), BF16),
            pltpu.VMEM((CAP + 1, R, TILE), F32),
            pltpu.VMEM(block, F32),
            pltpu.VMEM(block, F32),
            pltpu.VMEM(block, BF16),
            pltpu.VMEM(block, BF16),
            pltpu.VMEM(block, F32),
            pltpu.VMEM(block, F32),
            pltpu.VMEM(block, F32),
            pltpu.VMEM((PASSES, *block), F32),
            pltpu.VMEM((PASSES, *block), F32),
            pltpu.VMEM(block, F32),
            pltpu.VMEM((1 + PASSES, 18, R // 2, 2 * R), F32),
            pltpu.VMEM((PASSES, 4, R // 2, 2 * R), F32),
            pltpu.VMEM((PASSES, 22, 16, TILE), F32),
            pltpu.VMEM((PASSES, 2, 22, 8, TILE), F32),
            pltpu.VMEM((PASSES, 2, 6, 2, R, TILE), F32),
            pltpu.VMEM((PASSES, 16, R, TILE), F32),
            pltpu.VMEM((PASSES, 15, R, TILE), F32),
            pltpu.VMEM((8, CAP), jnp.int32),
            pltpu.VMEM((8, TILE), jnp.int32),
            pltpu.SMEM((8, CAP), jnp.int32),
            pltpu.SMEM((8, TILE), jnp.int32),
            pltpu.SemaphoreType.DMA,
            pltpu.SemaphoreType.DMA((2,)),
            pltpu.SemaphoreType.DMA((3,)),
            pltpu.SemaphoreType.DMA((2,)),
            pltpu.SemaphoreType.DMA((GROUPS,)),
            pltpu.SemaphoreType.DMA((GROUPS,)),
        ],
        compiler_params=pltpu.CompilerParams(
            collective_id=0, has_side_effects=True, vmem_limit_bytes=63 * 1024 * 1024
        ),
    )(tile_index, tile_count, tile_values, user_prev, item_prev, day_prior.T)
    users, items, days = copied(results)
    return users, items, days.T


def solution(mesh):
    return jax.shard_map(
        shards,
        mesh=mesh,
        in_specs=(
            P(("au", "ia"), None, None),
            P(None, ("au", "ia")),
            P(("au", "ia")),
            P(None, "au"),
            P(None, "ia"),
            P(),
        ),
        out_specs=(P(None, "au"), P(None, "ia"), P()),
        check_vma=False,
    )
```

```python
import functools

import jax
import jax.numpy as jnp
from jax import lax
from jax.experimental import pallas as pl
from jax.experimental.pallas import tpu as pltpu
from jax.sharding import PartitionSpec as P

PASSES = 2
R = 64
TILE = 128
DAYS = 32
BLOCKS = 32
CAP = 256
EPSILON = 1e-06
USER_ENTRIES = 64 * 131072
ITEM_ENTRIES = 64 * 16384
UNROLL = 128
MESH = pl.DeviceIdType.MESH
F32 = jnp.float32
BF16 = jnp.bfloat16

NN = (((1,), (0,)), ((), ()))
NT = (((1,), (1,)), ((), ()))


def mm(left, right, dims=NN):
    return lax.dot_general(left, right, dims, preferred_element_type=F32)


def halves(values):
    high = values.astype(BF16)
    return high, (values - high.astype(F32)).astype(BF16)


def left_three(values):
    high, low = halves(values)
    return jnp.concatenate([high, high, low], axis=1)


def right_three(values):
    high, low = halves(values)
    return jnp.concatenate([high, low, high], axis=0)


def drain(job):
    for _ in job:
        pass


class Group:
    def __init__(self, sems):
        self.send, self.recv = sems

    def start(self, source, target, device):
        pltpu.make_async_remote_copy(
            src_ref=source,
            dst_ref=target,
            send_sem=self.send,
            recv_sem=self.recv,
            device_id=device,
            device_id_type=MESH,
        ).start()

    def wait(self, all_of_it):
        pltpu.make_async_copy(all_of_it, all_of_it, self.recv).wait()
        pltpu.make_async_copy(all_of_it, all_of_it, self.send).wait()


class Groups:
    def __init__(self, send, recv):
        self.send, self.recv, self.used = send, recv, 0

    def new(self):
        self.used += 1
        return Group((self.send.at[self.used - 1], self.recv.at[self.used - 1]))


GROUPS = 2 + (3 + 1 + 3 + 3 + 3 + 4 + 4 + 4 + 1 + 15 + 1)


def order_slots(index, live, codes, last):
    slot = lax.broadcasted_iota(jnp.int32, (8, CAP), 1)
    rows = jnp.concatenate([index[...], jnp.zeros((5, CAP), jnp.int32)], axis=0)
    keys = jnp.where(slot < live, rows, BLOCKS)
    unique = keys * CAP + slot
    unique_down = unique.T
    code = slot[:1] + rows[:1] * 256 + rows[1:2] * 8192 + rows[2:3] * 262144
    ranks = [
        jnp.sum(jnp.where(unique_down[:, k : k + 1] < unique[k : k + 1], 1, 0), axis=0, keepdims=True)
        for k in range(3)
    ]
    down = jnp.concatenate(ranks + [code, slot[:4]], axis=0).T
    keys_down = keys.T
    place = lax.broadcasted_iota(jnp.int32, (CAP, CAP), 1)
    block = lax.broadcasted_iota(jnp.int32, (CAP, TILE), 1)
    for k in range(3):
        chosen = jnp.where(down[:, k : k + 1] == place, down[:, 3:4], 0)
        chosen = jnp.sum(chosen, axis=0, keepdims=True)
        key = jnp.where(slot[:1] < live, (chosen >> (8 + 5 * k)) & 31, BLOCKS)
        starts = (slot[:1] == 0) | (key != pltpu.roll(key, 1, 1))
        codes[k : k + 1, :] = chosen + jnp.where(starts, 1 << 23, 0)
        upto = jnp.sum(jnp.where(keys_down[:, k : k + 1] <= block, 1, 0), axis=0, keepdims=True)
        count = jnp.sum(jnp.where(keys_down[:, k : k + 1] == block, 1, 0), axis=0, keepdims=True)
        last[k : k + 1, :] = jnp.where(count > 0, upto - 1, CAP)


def kernel(
    index, live_count, tiles_hbm, user_hbm, item_hbm, day_prior,
    user_out, item_out, day_out,
    user_prior, item_prior,
    tiles, tiles_t, running, users, items, users_half, items_half, spread,
    mu, mi, t1u, t1i, t2,
    gu_slots, gv_slots, md_slots, scale_slots, urecv, irecv_core, irecv,
    codes_made, last_made, codes, last,
    tile_sem, prior_sem, out_sem, order_sem, send, recv,
):
    au = lax.axis_index("au")
    x = lax.axis_index("ia")
    core = lax.rem(au, 2)
    z = lax.rem(lax.div(au, 2), 4)
    y = lax.div(au, 8)
    plane = y * 4 + z

    def at(yy, zz, cc):
        return (yy * 4 + zz) * 2 + cc

    twin = (at(y, z, 1 - core), x)

    def along_x(step):
        return (au, lax.rem(x + step, 4))

    def along_y(step):
        return (at(lax.rem(y + step, 4), z, core), x)

    def along_z(step):
        return (at(y, lax.rem(z + step, 4), core), x)

    far_first = (2, 1, 3, 0)

    def along_yz(step):
        yy, zz = lax.rem(y + step // 4, 4), lax.rem(z + step % 4, 4)
        return (at(yy, zz, core), x)

    def plane_of(step):
        return lax.rem(y + step // 4, 4) * 4 + lax.rem(z + step % 4, 4)

    kinds = {
        "core": (2, core, lambda step: twin),
        "x": (4, x, along_x),
        "y": (4, y, along_y),
        "z": (4, z, along_z),
        "yz": (16, plane, along_yz),
    }

    def distance(step):
        return (0, 1, 2, 1)[step // 4] + (0, 1, 2, 1)[step % 4]

    orders = {
        2: (1,),
        4: (2, 1, 3),
        16: sorted(range(1, 16), key=lambda step: -distance(step)),
    }

    groups = Groups(send, recv)

    tile_copy = pltpu.make_async_copy(tiles_hbm, tiles, tile_sem)
    prior_copies = [
        pltpu.make_async_copy(user_hbm, user_prior, prior_sem.at[0]),
        pltpu.make_async_copy(item_hbm, item_prior, prior_sem.at[1]),
    ]
    for copy in prior_copies:
        copy.start()
    tile_copy.start()

    barrier = pltpu.get_barrier_semaphore()
    peers = [twin] + [along_x(step) for step in (1, 2, 3)] + [along_yz(step) for step in range(1, 16)]
    for peer in peers:
        pl.semaphore_signal(barrier, inc=1, device_id=peer, device_id_type=MESH)

    def total_over(stages, where, value, result):
        base = 0
        for stage in stages:
            size, mine, along = kinds[stage]
            here = where.at[base + mine]
            where[base + mine] = value
            group = groups.new()
            for step in orders[size]:
                group.start(here, here, along(step))
            yield
            group.wait(where.at[pl.ds(base, size - 1)])
            terms = [where[base + place] for place in range(size)]
            while len(terms) > 1:
                terms = [terms[k] + terms[k + 1] for k in range(0, len(terms), 2)]
            value = terms[0]
            base += size
        result.append(value)

    def ring_part(share, piece):
        return pl.ds(lax.rem(share, 4) * 8 + 2 * piece, 2)

    def reduce_ring(source, part, got):
        first, second = 2 * part, 2 * part + 1
        far, right, left = x + 2, x + 1, x + 3
        distant, close = groups.new(), groups.new()
        distant.start(source.at[ring_part(far, first)], got.at[0], along_x(3))
        distant.start(source.at[ring_part(far, second)], got.at[1], along_x(1))
        yield
        close.start(source.at[ring_part(left, second)], got.at[2], along_x(3))
        close.start(source.at[ring_part(right, first)], got.at[3], along_x(1))
        yield
        distant.wait(got.at[pl.ds(0, 2)])
        here = ring_part(left, first)
        source[here] = source[here] + got[0]
        close.start(source.at[here], got.at[4], along_x(3))
        there = ring_part(right, second)
        source[there] = source[there] + got[1]
        close.start(source.at[there], got.at[5], along_x(1))
        yield
        close.wait(got.at[pl.ds(2, 4)])
        mine = ring_part(x, first)
        source[mine] = source[mine] + (got[4] + got[3])
        mine = ring_part(x, second)
        source[mine] = source[mine] + (got[2] + got[5])

    def gather_ring(source, part):
        def piece(share, which):
            return source.at[ring_part(share, 2 * part + which)]

        left, right = x + 3, x + 1
        onward, rest = groups.new(), groups.new()
        onward.start(piece(x, 0), piece(x, 0), along_x(1))
        onward.start(piece(x, 1), piece(x, 1), along_x(3))
        rest.start(piece(x, 1), piece(x, 1), along_x(1))
        rest.start(piece(x, 0), piece(x, 0), along_x(3))
        yield
        onward.wait(source.at[pl.ds(0, 4)])
        rest.start(piece(left, 0), piece(left, 0), along_x(1))
        rest.start(piece(right, 1), piece(right, 1), along_x(3))
        yield
        rest.wait(source.at[pl.ds(0, 8)])

    def row_of(step):
        return pl.ds(lax.rem(y + step, 4) * 4, 4)

    def reduce_plane(source, got_core, got):
        own, other = core * 16, 16 - core * 16
        between = []
        for row in far_first:
            place = row_of(row)
            group = groups.new()
            group.start(source.at[pl.ds(other + place.start, 4)], got_core.at[place], twin)
            between.append((row, group))
        yield
        flying = groups.new()
        for row, group in between:
            place = row_of(row)
            group.wait(got_core.at[place])
            here = pl.ds(own + place.start, 4)
            source[here] = source[here] + got_core[place]
            for step in (row * 4 + further for further in far_first):
                if step:
                    flying.start(source.at[own + plane_of(step)], got.at[step - 1], along_yz(step))
        yield
        flying.wait(got)
        total = source[own + plane]
        for step in range(15):
            total = total + got[step]
        source[own + plane] = total

    def gather_plane(source):
        own = core * 16
        here = source.at[own + plane]
        flying = {step: groups.new() for step in orders[16]}
        for step in orders[16]:
            flying[step].start(here, here, along_yz(step))
        yield
        between = groups.new()
        between.start(here, here, twin)
        for step in reversed(orders[16]):
            back = (4 - step // 4) % 4 * 4 + (4 - step % 4) % 4
            place = source.at[own + plane_of(back)]
            flying[step].wait(place)
            between.start(place, place, twin)
        yield
        between.wait(source.at[pl.ds(0, 16)])

    def inverse(gram):
        rows = lax.broadcasted_iota(jnp.int32, (R, 2 * R), 0)
        lanes = lax.broadcasted_iota(jnp.int32, (R, 2 * R), 1)
        diagonal = jnp.where(rows == lanes, 1.0, 0.0)
        trace = jnp.sum(jnp.sum(gram * diagonal[:, :R], axis=1, keepdims=True), axis=0, keepdims=True)
        matrix = gram / (trace / R) + 0.1 * diagonal[:, :R]
        matrix = jnp.concatenate([matrix, diagonal[:, :R]], axis=1)

        place = rows[:8]

        def wide(column):
            return jnp.broadcast_to(column, (8, 2 * R))

        def eight(_, matrix):
            top = matrix[:8]
            columns = [wide(top[:, k : k + 1]) for k in range(8)]
            for k in range(8):
                share = 1.0 / columns[k][k : k + 1]
                column = (columns[k] - jnp.where(place == k, 1.0, 0.0)) * share
                top = top - column * top[k : k + 1]
                for j in range(k + 1, 8):
                    columns[j] = columns[j] - column * columns[j][k : k + 1]
            rest = []
            for begin in range(8, R, 8):
                value = matrix[begin : begin + 8]
                terms = [wide(value[:, k : k + 1]) * top[k : k + 1] for k in range(8)]
                while len(terms) > 1:
                    terms = [terms[k] + terms[k + 1] for k in range(0, len(terms), 2)]
                rest.append(value - terms[0])
            return pltpu.roll(jnp.concatenate(rest + [top], axis=0), 2 * R - 8, 1)

        return left_three(lax.fori_loop(0, R // 8, eight, matrix)[:, :R])

    def place_of(order, place):
        code = codes[order, place]
        keep = (1 - (code >> 23)).astype(F32)
        return code & 255, (code >> 8) & 31, (code >> 13) & 31, (code >> 18) & 31, keep

    def sweep(order, product, begin=0, end=CAP, acc=None):
        def visit(turn, acc):
            for k in range(UNROLL):
                place = turn * UNROLL + k
                *chosen, keep = place_of(order, place)
                acc = acc * keep + product(place, *chosen)
                running[place] = acc
            return acc

        if acc is None:
            acc = jnp.zeros((R, TILE), F32)
        return lax.fori_loop(begin // UNROLL, end // UNROLL, visit, acc)

    def day_partials(begin, end):
        def visit(turn, carry):
            for k in range(UNROLL):
                place = turn * UNROLL + k
                slot, ub, _, _, _ = place_of(2, place)
                running[place] = mm(users_half[ub], tiles[slot])
            return carry

        lax.fori_loop(begin // UNROLL, end // UNROLL, visit, 0)

    def each_block(visit, by=4, begin=0, count=BLOCKS):
        def some(step, carry):
            for k in range(by):
                visit(begin + step * by + k)
            return carry

        lax.fori_loop(0, count // by, some, 0)

    def columns(block):
        return pl.ds(pl.multiple_of(block * TILE, TILE), TILE)

    def assemble(order, target, begin=0, count=BLOCKS):
        def visit(block):
            target[block] = running[last[order, block]]

        each_block(visit, 8, begin, count)

    def gram_of(source):
        def eight(step, carry):
            total, cross = carry
            for k in range(4):
                block = step * 8 + k * 2
                high, low = halves(jnp.concatenate([source[block], source[block + 1]], axis=1))
                total = total + mm(high, high, NT)
                cross = cross + mm(high, low, NT)
            return total, cross

        zero = jnp.zeros((R, R), F32)
        total, cross = lax.fori_loop(0, BLOCKS // 8, eight, (zero, zero))
        return total + (cross + cross.T)

    def fold(gram):
        return jnp.concatenate([gram[: R // 2], gram[R // 2 :]], axis=1)

    def unfold(value):
        return jnp.concatenate([value[:, :R], value[:, R:]], axis=0)

    def squares(source, begin, count):
        total = jnp.zeros((8, TILE), F32)
        for step in range(count):
            value = source[begin + step]
            value = value * value
            total = total + jnp.sum(value.reshape(8, 8, TILE), axis=0)
        return total

    def scale_of(total, entries):
        total = jnp.sum(jnp.sum(total, axis=1, keepdims=True), axis=0, keepdims=True)
        return jnp.sqrt(total / entries + EPSILON)

    def prior_part(inv, prior):
        def visit(step, carry):
            wide = prior[:, pl.ds(pl.multiple_of(step * 4 * TILE, 4 * TILE), 4 * TILE)]
            wide = mm(inv, right_three(wide))
            for k in range(4):
                t2[step * 4 + k] = wide[:, k * TILE : (k + 1) * TILE]
            return carry

        lax.fori_loop(0, BLOCKS // 4, visit, 0)

    def apply(inv, source, begin, count, target):
        for step in range(count):
            target[begin + step] = mm(inv, right_three(source[begin + step]))

    def finish(target, target_half, t1, norm, out=None, begin=0, count=BLOCKS):
        share = 1.0 / norm

        def visit(block):
            value = t1[block] * share + t2[block]
            target[block] = value
            target_half[block] = value.astype(BF16)
            if out is not None:
                out[:, columns(block)] = value

        each_block(visit, 8, begin, count)

    order_slots(index, live_count[0], codes_made, last_made)
    codes_copy = pltpu.make_async_copy(codes_made, codes, order_sem.at[0])
    last_copy = pltpu.make_async_copy(last_made, last, order_sem.at[1])
    codes_copy.start()
    last_copy.start()

    def lay(block):
        value = user_prior[:, columns(block)]
        users[block] = value
        users_half[block] = value.astype(BF16)
        value = item_prior[:, columns(block)]
        items[block] = value
        items_half[block] = value.astype(BF16)

    for copy in prior_copies:
        copy.wait()
    each_block(lay)
    running[CAP] = jnp.zeros((R, TILE), F32)
    gu_part = fold(gram_of(users))
    day_rows = day_prior[...].T
    lanes = lax.broadcasted_iota(jnp.int32, (R, TILE), 1)

    def transpose_tiles(begin, end):
        def visit(step, carry):
            for k in range(16):
                tiles_t[step * 16 + k] = tiles[step * 16 + k].T
            return carry

        lax.fori_loop(begin // 16, end // 16, visit, 0)

    gu_found = []
    gu_job = total_over(("core", "yz"), gu_slots.at[0], gu_part, gu_found)

    for turn in range(PASSES):
        groups.used = 0
        final = turn == PASSES - 1

        if turn == 0:
            tile_copy.wait()
            codes_copy.wait()
            last_copy.wait()

        def day_product(place, slot, ub, ib, day):
            if turn == 0:
                return mm(users_half[ub], tiles[slot]) * items_half[ib].astype(F32)
            return running[place] * items_half[ib].astype(F32)

        if turn == 0:
            acc = sweep(2, day_product, 0, CAP // 2)
            pl.semaphore_wait(barrier, len(peers))
            next(gu_job)
            sweep(2, day_product, CAP // 2, CAP, acc)
            next(gu_job)
        else:
            sweep(2, day_product)

        def day_sums(step, total):
            for k in range(16):
                day = step * 16 + k
                value = jnp.sum(running[last[2, day]], axis=1, keepdims=True)
                total = jnp.where(lanes == day, value, total)
            return total

        moments = lax.fori_loop(0, DAYS // 16, day_sums, jnp.zeros((R, TILE), F32))
        moments = (moments[:16] + pltpu.roll(moments[16:32], 32, 1)) + (
            pltpu.roll(moments[32:48], 64, 1) + pltpu.roll(moments[48:], 96, 1)
        )
        md_found = []
        md_job = total_over(("core", "x", "yz"), md_slots.at[turn], moments, md_found)
        next(md_job)
        gv_found = []
        gv_job = total_over(("x",), gv_slots.at[turn], fold(gram_of(items)), gv_found)
        next(gv_job)
        next(md_job)
        if turn == 0:
            transpose_tiles(0, CAP)
            drain(gu_job)
            gram_users = unfold(gu_found[0])
        drain(gv_job)
        gram_items = unfold(gv_found[0])
        next(md_job)
        inv = inverse(gram_users * gram_items)
        ahead = mm(inv, right_three(day_rows))
        drain(md_job)
        moments = md_found[0]
        square = moments * moments
        square = jnp.sum(jnp.sum(square, axis=1, keepdims=True), axis=0, keepdims=True)
        norm = jnp.sqrt(square / (R * DAYS) + EPSILON)
        moments = jnp.concatenate(
            [moments[:, :DAYS]] + [pltpu.roll(moments, TILE - k * 32, 1)[:, :DAYS] for k in (1, 2, 3)], axis=0
        )
        days = mm(inv, right_three(moments)) * (1.0 / norm) + ahead
        for day in range(DAYS):
            spread[day] = jnp.broadcast_to(days[:, day : day + 1], (R, TILE))
        if final:
            day_out[...] = days.T

        def user_product(place, slot, ub, ib, day):
            return mm((items[ib] * spread[day]).astype(BF16), tiles_t[slot])

        sweep(0, user_product)
        assemble(0, mu, lax.rem(x + 2, 4) * 8, 8)
        parts = [reduce_ring(mu, part, urecv.at[turn, part]) for part in range(2)]
        next(parts[0])
        for share in (x + 1, x + 3, x):
            assemble(0, mu, lax.rem(share, 4) * 8, 8)
        next(parts[0])
        next(parts[1])
        high, low = halves(days)
        cross = mm(high, low, NT)
        gram_days = mm(high, high, NT) + (cross + mm(low, high, NT))
        inv = inverse(gram_items * gram_days)
        next(parts[0])
        next(parts[1])
        next(parts[1])
        jobs = []
        for part in range(2):
            drain(parts[part])
            apply(inv, mu, x * 8 + 4 * part, 4, t1u.at[turn])
            jobs.append(gather_ring(t1u.at[turn], part))
            next(jobs[part])
        scale_found = []
        scale_job = total_over(
            ("core", "yz", "x"), scale_slots.at[turn, 0], squares(mu, x * 8, 8), scale_found
        )
        next(scale_job)
        next(scale_job)
        next(jobs[0])
        prior_part(inv, user_prior)
        next(jobs[1])
        next(scale_job)
        drain(scale_job)
        for job in jobs:
            drain(job)
        norm = scale_of(scale_found[0], USER_ENTRIES)
        finish(users, users_half, t1u.at[turn], norm, user_prior if final else None)
        if final:
            user_copy = pltpu.make_async_copy(user_prior, user_out, out_sem.at[0])
            user_copy.start()

        gu_found = []
        gu_job = total_over(("core", "y", "z"), gu_slots.at[1 + turn], fold(gram_of(users)), gu_found)
        next(gu_job)

        def item_product(place, slot, ub, ib, day):
            return mm((users[ub] * spread[day]).astype(BF16), tiles[slot])

        acc = sweep(1, item_product, 0, CAP // 2)
        next(gu_job)
        sweep(1, item_product, CAP // 2, CAP, acc)
        assemble(1, mi, 16 - core * 16, 16)
        job = reduce_plane(mi, irecv_core.at[turn], irecv.at[turn])
        next(job)
        assemble(1, mi, core * 16, 16)
        next(job)
        if not final:
            day_partials(0, CAP // 2)
        next(gu_job)
        if not final:
            day_partials(CAP // 2, CAP)
        drain(gu_job)
        gram_users = unfold(gu_found[0])
        inv = inverse(gram_users * gram_days)
        drain(job)
        scale_found = []
        scale_job = total_over(
            ("yz", "core", "x"), scale_slots.at[turn, 1], squares(mi, core * 16 + plane, 1), scale_found
        )
        next(scale_job)
        apply(inv, mi, core * 16 + plane, 1, t1i.at[turn])
        job = gather_plane(t1i.at[turn])
        next(job)
        prior_part(inv, item_prior)
        next(scale_job)
        next(scale_job)
        next(job)
        drain(scale_job)
        norm = scale_of(scale_found[0], ITEM_ENTRIES)
        out = item_prior if final else None
        item_copies = []
        for part, begin in enumerate((core * 16, 16 - core * 16)):
            if part == 1:
                drain(job)
            finish(items, items_half, t1i.at[turn], norm, out, begin, 16)
            if final:
                half = pl.ds(pl.multiple_of(begin * TILE, 16 * TILE), 16 * TILE)
                copy = pltpu.make_async_copy(item_prior.at[:, half], item_out.at[:, half], out_sem.at[1 + part])
                copy.start()
                item_copies.append(copy)

    user_copy.wait()
    for copy in item_copies:
        copy.wait()


PIECES = 4


def copy_kernel(user_in, item_in, day_in, user_out, item_out, day_out, user_held, item_held, day_held, sem):
    jobs = [(day_in, day_held, day_out)]
    for source, held, target in ((user_in, user_held, user_out), (item_in, item_held, item_out)):
        size = R // PIECES
        for k in range(PIECES):
            rows = pl.ds(k * size, size)
            jobs.append((source.at[rows], held.at[rows], target.at[rows]))
    arriving = [pltpu.make_async_copy(one[0], one[1], sem.at[0, k]) for k, one in enumerate(jobs)]
    leaving = [pltpu.make_async_copy(one[1], one[2], sem.at[1, k]) for k, one in enumerate(jobs)]
    for copy in arriving:
        copy.start()
    for copy, onward in zip(arriving, leaving):
        copy.wait()
        onward.start()
    for copy in leaving:
        copy.wait()


def copied(arrays):
    anywhere = pl.BlockSpec(memory_space=pl.ANY)
    return pl.pallas_call(
        copy_kernel,
        out_shape=tuple(jax.ShapeDtypeStruct(one.shape, one.dtype) for one in arrays),
        in_specs=[anywhere] * 3,
        out_specs=(anywhere,) * 3,
        scratch_shapes=[pltpu.VMEM(one.shape, one.dtype) for one in arrays]
        + [pltpu.SemaphoreType.DMA((2, 1 + 2 * PIECES))],
        compiler_params=pltpu.CompilerParams(vmem_limit_bytes=63 * 1024 * 1024),
    )(*arrays)


def shards(tile_values, tile_index, tile_count, user_prev, item_prev, day_prior):
    vmem = pl.BlockSpec(memory_space=pltpu.VMEM)
    smem = pl.BlockSpec(memory_space=pltpu.SMEM)
    anywhere = pl.BlockSpec(memory_space=pl.ANY)
    block = (BLOCKS, R, TILE)
    results = pl.pallas_call(
        kernel,
        out_shape=(
            jax.ShapeDtypeStruct(user_prev.shape, F32),
            jax.ShapeDtypeStruct(item_prev.shape, F32),
            jax.ShapeDtypeStruct(day_prior.shape[::-1], F32),
        ),
        in_specs=[vmem, smem, anywhere, anywhere, anywhere, vmem],
        out_specs=(anywhere, anywhere, vmem),
        scratch_shapes=[
            pltpu.VMEM(user_prev.shape, F32),
            pltpu.VMEM(item_prev.shape, F32),
            pltpu.VMEM((CAP, TILE, TILE), BF16),
            pltpu.VMEM((CAP, TILE, TILE), BF16),
            pltpu.VMEM((CAP + 1, R, TILE), F32),
            pltpu.VMEM(block, F32),
            pltpu.VMEM(block, F32),
            pltpu.VMEM(block, BF16),
            pltpu.VMEM(block, BF16),
            pltpu.VMEM(block, F32),
            pltpu.VMEM(block, F32),
            pltpu.VMEM(block, F32),
            pltpu.VMEM((PASSES, *block), F32),
            pltpu.VMEM((PASSES, *block), F32),
            pltpu.VMEM(block, F32),
            pltpu.VMEM((1 + PASSES, 18, R // 2, 2 * R), F32),
            pltpu.VMEM((PASSES, 4, R // 2, 2 * R), F32),
            pltpu.VMEM((PASSES, 22, 16, TILE), F32),
            pltpu.VMEM((PASSES, 2, 22, 8, TILE), F32),
            pltpu.VMEM((PASSES, 2, 6, 2, R, TILE), F32),
            pltpu.VMEM((PASSES, 16, R, TILE), F32),
            pltpu.VMEM((PASSES, 15, R, TILE), F32),
            pltpu.VMEM((8, CAP), jnp.int32),
            pltpu.VMEM((8, TILE), jnp.int32),
            pltpu.SMEM((8, CAP), jnp.int32),
            pltpu.SMEM((8, TILE), jnp.int32),
            pltpu.SemaphoreType.DMA,
            pltpu.SemaphoreType.DMA((2,)),
            pltpu.SemaphoreType.DMA((3,)),
            pltpu.SemaphoreType.DMA((2,)),
            pltpu.SemaphoreType.DMA((GROUPS,)),
            pltpu.SemaphoreType.DMA((GROUPS,)),
        ],
        compiler_params=pltpu.CompilerParams(
            collective_id=0, has_side_effects=True, vmem_limit_bytes=63 * 1024 * 1024
        ),
    )(tile_index, tile_count, tile_values, user_prev, item_prev, day_prior.T)
    users, items, days = copied(results)
    return users, items, days.T


def solution(mesh):
    return jax.shard_map(
        shards,
        mesh=mesh,
        in_specs=(
            P(("au", "ia"), None, None),
            P(None, ("au", "ia")),
            P(("au", "ia")),
            P(None, "au"),
            P(None, "ia"),
            P(),
        ),
        out_specs=(P(None, "au"), P(None, "ia"), P()),
        check_vma=False,
    )
```
